256 devices in a mesh: dp: 4 (over z_lo), ctx: 64 (over z_hi, y, x, core).
Axes of the slice: x: 4, y: 4, z: 8 (z_hi: 2, z_lo: 4; z = z_hi * 4 + z_lo), core: 2. Of those that a mesh axis runs over, the one named last changes fastest.
Arguments:
- qkv: bfloat16 [4, 8192, 6144], P('dp', 'ctx'), may hold values from -6 to 6
- short_filter: float32 [7, 768], replicated, may hold values from -2 to 2
- long_filter: float32 [2048, 8192], P('ctx'), may hold values from -1.1 to 1.1
- cotangent: bfloat16 [4, 8192, 2048], P('dp', 'ctx'), may hold values from -6 to 6
Outputs:
- mixer_out: bfloat16 [4, 8192, 2048], P('dp', 'ctx')
- grad_qkv: bfloat16 [4, 8192, 6144], P('dp', 'ctx')
- grad_long: float32 [2048, 8192], P('ctx')
- grad_short: float32 [7, 768], replicated
The draws below stay inside these ranges and needn't reach their ends.
All inputs are finite; a program needn't handle non-finite values.
Results may differ from the reference program's by a relative error of at most 0.014.
Values may be sent and summed in bfloat16 or wider, within the bound.
No kernel may reach another device: no remote copies, remote signals or barrier semaphores. Data moves between devices by JAX's collectives and lax.ppermute only.
A program may use at most 128 MiB of HBM per device.

```python
import math
import jax
import jax.numpy as jnp
from jax import lax

D = 2048
SHORT_GROUPS = 256
KSIZE = 7
SEQS = 4
LEN = 8192


def draw_long_filter(key, part):
    keys = jax.random.split(key, 6)
    lags = jnp.arange(LEN, dtype=jnp.float32)[None, :]
    slow_rate = jax.random.uniform(keys[0], (D, 1), jnp.float32, 0.1, 1.0) / LEN
    fast_rate = jax.random.uniform(keys[1], (D, 1), jnp.float32, 1.0 / 50.0, 1.0 / 30.0)
    share = 0.5
    noise = jnp.clip(jax.random.normal(keys[5], (D, LEN), jnp.float32), -4.0, 4.0)
    picker = jax.random.uniform(keys[2], (D, 1), jnp.float32)
    rate = jnp.where(picker < share, slow_rate, fast_rate)
    spots = jax.random.randint(keys[3], (D, 2), 1, LEN).astype(jnp.float32)
    drops = jax.random.uniform(keys[4], (D, 2), jnp.float32, 0.6, 0.85)
    envelope = jnp.exp(-rate * lags)
    envelope = envelope * jnp.where(lags >= spots[:, 0:1], drops[:, 0:1], 1.0)
    envelope = envelope * jnp.where(lags >= spots[:, 1:2], drops[:, 1:2], 1.0)
    norming = jnp.sqrt(1.0 - jnp.exp(-2.0 * rate))
    return (envelope * norming * noise).astype(jnp.float32)


def block_levels(stream_key, extent, shards, low, top_value):
    gain, own = 1.0, jax.random.fold_in(stream_key, 6)
    for axis_at, shards_of in shards:
        heights = jnp.exp(jax.random.uniform(jax.random.fold_in(own, axis_at), (shards_of,), jnp.float32, low / len(shards), top_value / len(shards)))
        gain = gain * jnp.repeat(heights, extent[axis_at] // shards_of).reshape([-1 if axis == axis_at else 1 for axis in range(len(extent))])
    return gain


def scatter_about(key, shape, spread, bound, cuts=(), kind=jnp.bfloat16):
    level = block_levels(key, shape, cuts, -0.22, 0.18) if cuts else 1.0
    array = jax.random.normal(key, shape, jnp.float32) * spread * level
    return jnp.minimum(jnp.maximum(array, -bound), bound).astype(kind)


def setup_inputs(seed: int = 0) -> dict:
    splits = jax.random.split(jax.random.key(seed), 5)
    qkv = scatter_about(splits[0], (SEQS, LEN, 3 * D), 1.0, 6.0, ((0, 4), (1, 64)))
    short_filter = scatter_about(splits[1], (KSIZE, 3 * SHORT_GROUPS), KSIZE ** -0.5, 2.0, (), jnp.float32)
    long_filter = draw_long_filter(jax.random.fold_in(splits[4], 71), 0)
    cotangent = scatter_about(splits[3], (SEQS, LEN, D), 1.0, 6.0, ((0, 4), (1, 64)))
    return {"qkv": qkv, "short_filter": short_filter, "long_filter": long_filter, "cotangent": cotangent}


def reference(qkv, short_filter, long_filter, cotangent):
    width_all = 3 * D
    tap_count = short_filter.shape[0]
    group_size = width_all // short_filter.shape[1]
    tap_weights = jnp.repeat(short_filter, group_size, axis=1)
    length = qkv.shape[1]
    padded_len = 2 * length
    grad_scale = 1.0 / math.sqrt(qkv.shape[0] * length)
    filter_spec = jnp.fft.rfft(long_filter.T, n=padded_len, axis=0)

    def per_sequence(running, inputs):
        feats, cot_rows = inputs
        feats_wide = feats.astype(jnp.float32)
        padded = jnp.pad(feats_wide, ((tap_count - 1, 0), (0, 0)))
        short_out = jnp.zeros((length, width_all), jnp.float32)
        for lag_index in range(tap_count):
            start = tap_count - 1 - lag_index
            short_out = short_out + tap_weights[lag_index] * padded[start:start + length]
        query_rows = short_out[:, :D]
        key_rows = short_out[:, D:2 * D]
        value_rows = short_out[:, 2 * D:]
        product = (key_rows * value_rows).astype(jnp.bfloat16)
        prod_spec = jnp.fft.rfft(product.astype(jnp.float32), n=padded_len, axis=0)
        long_out = jnp.fft.irfft(prod_spec * filter_spec, n=padded_len, axis=0)[:length].astype(jnp.bfloat16)
        long_wide = long_out.astype(jnp.float32)
        cot_wide = cot_rows.astype(jnp.float32)
        mixer_out = (query_rows * long_wide).astype(jnp.bfloat16)
        grad_in = (cot_wide * query_rows).astype(jnp.bfloat16)
        grad_spec = jnp.fft.rfft(grad_in.astype(jnp.float32), n=padded_len, axis=0)
        grad_product = jnp.fft.irfft(grad_spec * jnp.conj(filter_spec), n=padded_len, axis=0)[:length].astype(jnp.bfloat16)
        grad_taps = jnp.fft.irfft(grad_spec * jnp.conj(prod_spec), n=padded_len, axis=0)[:length]
        grad_wide = grad_product.astype(jnp.float32)
        grad_short_out = jnp.concatenate([cot_wide * long_wide, grad_wide * value_rows, grad_wide * key_rows], axis=1)
        grad_padded = jnp.pad(grad_short_out, ((0, tap_count - 1), (0, 0)))
        grad_rows = jnp.zeros((length, width_all), jnp.float32)
        for lag_index in range(tap_count):
            grad_rows = grad_rows + tap_weights[lag_index] * grad_padded[lag_index:lag_index + length]
        lag_terms = []
        for lag_index in range(tap_count):
            start = tap_count - 1 - lag_index
            lag_terms.append(lax.optimization_barrier(jnp.sum(grad_short_out * padded[start:start + length], axis=0)))
        short_terms = jnp.stack(lag_terms).reshape(tap_count, -1, group_size).sum(axis=2)
        long_acc, short_acc = running
        running = (long_acc + grad_taps.T * grad_scale, short_acc + short_terms * grad_scale)
        return (running, (mixer_out, grad_rows.astype(jnp.bfloat16)))
    start_state = (jnp.zeros((D, length), jnp.float32), jnp.zeros(short_filter.shape, jnp.float32))
    (grad_long, grad_short), (mixer_out, grad_qkv) = lax.scan(per_sequence, start_state, (qkv, cotangent))
    return (mixer_out, grad_qkv, grad_long, grad_short)
```

```python
import functools
import math

import jax
import jax.numpy as jnp
import numpy as np
from jax import lax
from jax.experimental import pallas as pl
from jax.experimental.pallas import tpu as pltpu
from jax.sharding import PartitionSpec as P

F32 = jnp.float32
BF16 = jnp.bfloat16
LANES = 128
OWN = 8
HALO = 8
ROT = -0.25
VMEM_LIMIT = 56 * 1024 * 1024


def two_parts(table):
    high = jnp.asarray(table, F32).astype(BF16)
    low = (jnp.asarray(table, F32) - high.astype(F32)).astype(BF16)
    return high, low


def make_tables(rows, cols):
    total = rows * cols
    k1 = np.arange(rows, dtype=np.float64)[:, None] + ROT
    n1 = np.arange(rows, dtype=np.float64)[None, :]
    turn = 2.0 * np.pi * k1 * n1 / rows
    first = np.concatenate([np.cos(turn), -np.sin(turn)], axis=0)
    last = np.concatenate([np.cos(turn.T), -np.sin(turn.T)], axis=1) / total
    n2 = np.arange(cols, dtype=np.float64)
    twist = 2.0 * np.pi * k1 * n2[None, :] / total
    twist = np.concatenate([np.cos(twist), -np.sin(twist)], axis=1)
    inner = 2.0 * np.pi * ((n2[:, None] * n2[None, :]) % cols) / cols
    real, imag = np.cos(inner), -np.sin(inner)
    ahead = np.block([[real, imag], [-imag, real]])
    back = np.block([[real, -imag], [imag, real]])
    first = jnp.concatenate(two_parts(first), axis=1)
    last = jnp.concatenate(two_parts(last), axis=1)
    ahead = jnp.concatenate(two_parts(ahead), axis=0)
    back = jnp.concatenate(two_parts(back), axis=0)
    return first, last, jnp.asarray(twist, F32), ahead, back


def mxu(left, right):
    return jnp.dot(left, right, preferred_element_type=F32)


def twice(array, axis):
    return jnp.concatenate([array, array], axis=axis)


def to_spectra(signals, first, twist, ahead):
    rows, cols = signals[0].shape
    wide = jnp.concatenate(signals, axis=1).astype(BF16)
    mixed = mxu(first, twice(wide, 0))
    twist_real, twist_imag = twist[:, :cols], twist[:, cols:]
    turned = []
    for at in range(len(signals)):
        real = mixed[:rows, at * cols : (at + 1) * cols]
        imag = mixed[rows:, at * cols : (at + 1) * cols]
        turned.append(
            jnp.concatenate(
                [real * twist_real - imag * twist_imag, real * twist_imag + imag * twist_real], axis=1
            )
        )
    turned = jnp.concatenate(turned, axis=0).astype(BF16)
    return mxu(twice(turned, 1), ahead)


def from_spectra(spectra, last, twist, back):
    rows, cols = spectra[0].shape[0], spectra[0].shape[1] // 2
    tall = jnp.concatenate(spectra, axis=0).astype(BF16)
    mixed = mxu(twice(tall, 1), back)
    twist_real, twist_imag = twist[:, :cols], twist[:, cols:]
    turned = []
    for at in range(len(spectra)):
        real = mixed[at * rows : (at + 1) * rows, :cols]
        imag = mixed[at * rows : (at + 1) * rows, cols:]
        turned.append(
            jnp.concatenate(
                [real * twist_real + imag * twist_imag, imag * twist_real - real * twist_imag], axis=0
            )
        )
    turned = jnp.concatenate(turned, axis=1).astype(BF16)
    return mxu(last, twice(turned, 0))


def times(left, right, flip):
    cols = left.shape[1] // 2
    left_real, left_imag = left[:, :cols], left[:, cols:]
    right_real, right_imag = right[:, :cols], right[:, cols:]
    if flip:
        real = left_real * right_real + left_imag * right_imag
        imag = left_imag * right_real - left_real * right_imag
    else:
        real = left_real * right_real - left_imag * right_imag
        imag = left_real * right_imag + left_imag * right_real
    return jnp.concatenate([real, imag], axis=1)


def filter_kernel(rows, place_ref, taps_ref, first_ref, twist_ref, ahead_ref, out_ref, spread):
    base = pl.multiple_of(place_ref[0] * OWN, OWN)
    for row in range(rows):
        spread[row * OWN : (row + 1) * OWN, :] = taps_ref[
            pl.ds(base, OWN), row * LANES : (row + 1) * LANES
        ]
    first, twist, ahead = first_ref[...], twist_ref[...], ahead_ref[...]
    twist_real, twist_imag = twist[:, :LANES], twist[:, LANES:]
    for half in range(2):
        wide = jnp.concatenate(
            [spread[pl.ds(half * 4 + at, rows, stride=OWN), :] for at in range(4)], axis=1
        )
        high = wide.astype(BF16)
        low = (wide - high.astype(F32)).astype(BF16)
        mixed = mxu(first, twice(high, 0)) + mxu(first[:, :rows], low)
        turned = []
        for at in range(4):
            real = mixed[:rows, at * LANES : (at + 1) * LANES]
            imag = mixed[rows:, at * LANES : (at + 1) * LANES]
            turned.append(
                jnp.concatenate(
                    [real * twist_real - imag * twist_imag, real * twist_imag + imag * twist_real],
                    axis=1,
                )
            )
        turned = jnp.concatenate(turned, axis=0)
        high = turned.astype(BF16)
        low = (turned - high.astype(F32)).astype(BF16)
        spectra = mxu(twice(high, 1), ahead) + mxu(low, ahead[: 2 * LANES])
        for at in range(4):
            out_ref[half * 4 + at] = spectra[at * rows : (at + 1) * rows]


def mix_kernel(
    seqs,
    rows,
    got_ref,
    filt_ref,
    first_ref,
    last_ref,
    twist_ref,
    ahead_ref,
    back_ref,
    out_ref,
    corr_ref,
    spread,
    gather,
):
    pair = 2 * OWN
    for seq in range(seqs):
        spread[seq * rows * pair : (seq + 1) * rows * pair, :] = (
            got_ref[seq].astype(F32).reshape(rows * pair, LANES)
        )
    first, last, twist = first_ref[...], last_ref[...], twist_ref[...]
    for chan in range(OWN):
        signals = [
            spread[pl.ds(seq * rows * pair + part * OWN + chan, rows, stride=pair), :]
            for part in range(2)
            for seq in range(seqs)
        ]
        spectra = to_spectra(signals, first, twist, ahead_ref[...])
        filt = filt_ref[chan]
        ahead_specs, back_specs, total = [], [], None
        for seq in range(seqs):
            prod = spectra[seq * rows : (seq + 1) * rows]
            grad = spectra[(seqs + seq) * rows : (seqs + seq + 1) * rows]
            ahead_specs.append(times(prod, filt, False))
            back_specs.append(times(grad, filt, True))
            term = times(grad, prod, True)
            total = term if total is None else total + term
        corr_ref[chan] = total
        result = from_spectra(ahead_specs + back_specs, last, twist, back_ref[...])
        at = 0
        for part in range(2):
            for seq in range(seqs):
                gather[pl.ds(seq * rows * pair + part * OWN + chan, rows, stride=pair), :] = result[
                    :, at * LANES : (at + 1) * LANES
                ]
                at += 1
    for seq in range(seqs):
        out_ref[seq] = (
            gather[seq * rows * pair : (seq + 1) * rows * pair, :]
            .reshape(rows, pair, LANES)
            .astype(BF16)
        )


def taps_kernel(rows, scale, corr_ref, last_ref, twist_ref, back_ref, out_ref, gather):
    last, twist, back = last_ref[...], twist_ref[...], back_ref[...]
    for half in range(2):
        result = from_spectra([corr_ref[half * 4 + at] for at in range(4)], last, twist, back)
        for at in range(4):
            gather[pl.ds(half * 4 + at, rows, stride=OWN), :] = (
                result[:, at * LANES : (at + 1) * LANES] * scale
            )
    for row in range(rows):
        out_ref[:, row * LANES : (row + 1) * LANES] = gather[row * OWN : (row + 1) * OWN, :].astype(BF16)


def join_kernel(place_ref, own_ref, one_ref, two_ref, three_ref, out_ref):
    place = place_ref[0]
    for step, ref in enumerate((own_ref, one_ref, two_ref, three_ref)):
        row = pl.multiple_of((place ^ step) * OWN, OWN)
        out_ref[pl.ds(row, OWN), :] = ref[...].astype(F32)


def group_table(groups, group_size):
    rows = lax.broadcasted_iota(jnp.int32, (groups, groups * group_size), 0)
    cols = lax.broadcasted_iota(jnp.int32, (groups, groups * group_size), 1)
    return jnp.where(cols // group_size == rows, 1.0, 0.0).astype(F32)


def spread_taps(taps_ref, group_size, wide):
    groups = taps_ref.shape[1]
    table = group_table(LANES, group_size)
    for at in range(groups // LANES):
        wide[:, at * LANES * group_size : (at + 1) * LANES * group_size] = jnp.dot(
            taps_ref[:, at * LANES : (at + 1) * LANES],
            table,
            precision=lax.Precision.HIGHEST,
            preferred_element_type=F32,
        )


def short_kernel(
    tap_count, group_size, qkv_ref, rim_ref, taps_ref, cot_ref, feats_ref, out_ref, padded, wide
):
    rows, width_all = qkv_ref.shape
    width = width_all // 3
    spread_taps(taps_ref, group_size, wide)
    padded[0:HALO, :] = rim_ref[...].astype(F32)
    padded[HALO : HALO + rows, :] = qkv_ref[...].astype(F32)
    per_chunk = LANES // OWN // 4

    def chunk(at, _):
        parts = []
        for part in range(3):
            cols = pl.ds(pl.multiple_of(part * width + at * LANES, LANES), LANES)
            total = wide[0:1, cols] * padded[HALO : HALO + rows, cols]
            for lag in range(1, tap_count):
                total = total + wide[lag : lag + 1, cols] * padded[HALO - lag : HALO - lag + rows, cols]
            feats_ref[:, cols] = total
            parts.append(total)
        cols = pl.ds(pl.multiple_of(at * LANES, LANES), LANES)
        product = (parts[1] * parts[2]).T.reshape(LANES // OWN, OWN, LANES)
        grad_in = (cot_ref[:, cols].astype(F32) * parts[0]).T.reshape(LANES // OWN, OWN, LANES)
        both = jnp.concatenate([product, grad_in], axis=1).astype(BF16)
        both = both.reshape(per_chunk, 4, 2 * OWN, LANES)
        for seq in range(4):
            out_ref[seq, pl.ds(at * per_chunk, per_chunk)] = both[:, seq]
        return 0

    lax.fori_loop(0, width // LANES, chunk, 0)


def gate_kernel(
    tap_count,
    group_size,
    scale,
    got_ref,
    feats_ref,
    cot_ref,
    qkv_ref,
    rim_ref,
    mixer_ref,
    gso_ref,
    edge_ref,
    short_ref,
    padded,
    sums,
):
    rows, width_all = qkv_ref.shape
    width = width_all // 3
    padded[0:HALO, :] = rim_ref[...].astype(F32)
    padded[HALO : HALO + rows, :] = qkv_ref[...].astype(F32)
    per_chunk = LANES // OWN // 4

    def chunk(at, _):
        both = jnp.stack(
            [got_ref[seq, pl.ds(at * per_chunk, per_chunk)] for seq in range(4)], axis=1
        ).astype(F32)
        both = both.reshape(LANES // OWN, 2 * OWN, LANES)
        long_out = both[:, :OWN].reshape(LANES, LANES).T
        grad_product = both[:, OWN:].reshape(LANES, LANES).T
        cols = [
            pl.ds(pl.multiple_of(part * width + at * LANES, LANES), LANES) for part in range(3)
        ]
        mixer_ref[:, cols[0]] = (feats_ref[:, cols[0]] * long_out).astype(BF16)
        grads = (
            cot_ref[:, cols[0]].astype(F32) * long_out,
            grad_product * feats_ref[:, cols[2]],
            grad_product * feats_ref[:, cols[1]],
        )
        for part in range(3):
            gso_ref[:, cols[part]] = grads[part]
            edge_ref[:, cols[part]] = grads[part][:HALO].astype(BF16)
            for lag in range(tap_count):
                term = grads[part] * padded[HALO - lag : HALO - lag + rows, cols[part]]
                sums[lag * 8 : (lag + 1) * 8, cols[part]] = jnp.sum(
                    term.reshape(rows // 8, 8, LANES), axis=0
                )
        return 0

    lax.fori_loop(0, width // LANES, chunk, 0)
    table = group_table(LANES, group_size)
    block = LANES * group_size
    for at in range(width_all // block):
        lags = [
            jnp.sum(sums[lag * 8 : (lag + 1) * 8, at * block : (at + 1) * block], axis=0, keepdims=True)
            for lag in range(tap_count)
        ]
        lags = jnp.concatenate(lags + [jnp.zeros((8 - tap_count, block), F32)], axis=0)
        short_ref[:, at * LANES : (at + 1) * LANES] = (
            lax.dot_general(
                lags,
                table,
                (((1,), (1,)), ((), ())),
                precision=lax.Precision.HIGHEST,
                preferred_element_type=F32,
            )
            * scale
        )


def back_kernel(tap_count, group_size, gso_ref, rim_ref, taps_ref, out_ref, padded, wide):
    rows, width_all = gso_ref.shape
    spread_taps(taps_ref, group_size, wide)
    padded[rows - HALO : rows, :] = gso_ref[rows - HALO : rows, :]
    padded[rows : rows + HALO, :] = rim_ref[...].astype(F32)
    body = rows - HALO

    def chunk(at, _):
        cols = pl.ds(pl.multiple_of(at * LANES, LANES), LANES)
        total = wide[0:1, cols] * gso_ref[0:body, cols]
        tail = wide[0:1, cols] * padded[body:rows, cols]
        for lag in range(1, tap_count):
            total = total + wide[lag : lag + 1, cols] * gso_ref[lag : lag + body, cols]
            tail = tail + wide[lag : lag + 1, cols] * padded[body + lag : rows + lag, cols]
        out_ref[:, cols] = jnp.concatenate([total, tail], axis=0).astype(BF16)
        return 0

    lax.fori_loop(0, width_all // LANES, chunk, 0)


def call(kernel, outs, scratch, args, cost, scalars=0):
    vmem = pl.BlockSpec(memory_space=pltpu.VMEM)
    smem = pl.BlockSpec(memory_space=pltpu.SMEM)
    flops, moved = (int(value) for value in cost)
    return pl.pallas_call(
        kernel,
        out_shape=outs,
        in_specs=[smem] * scalars + [vmem] * (len(args) - scalars),
        out_specs=jax.tree.map(lambda _: vmem, outs),
        scratch_shapes=scratch,
        compiler_params=pltpu.CompilerParams(vmem_limit_bytes=VMEM_LIMIT),
        cost_estimate=pl.CostEstimate(flops=flops, bytes_accessed=moved, transcendentals=0),
    )(*args)


def shape(dims, kind):
    return jax.ShapeDtypeStruct(dims, kind)


def neighbours(array, by):
    devices = lax.axis_size("ctx")
    pairs = [(i, i + by) for i in range(devices) if 0 <= i + by < devices]
    return lax.ppermute(array, "ctx", pairs)


def partner(array, axis, mask):
    return lax.ppermute(array, axis, [(i, i ^ mask) for i in range(lax.axis_size(axis))])


def shards(qkv, short_filter, long_filter, cotangent):
    feats_in, cot = qkv[0], cotangent[0]
    rows, width_all = feats_in.shape
    width = width_all // 3
    tap_count, groups = short_filter.shape
    group_size = width_all // groups
    seqs, ctx_count = lax.axis_size("dp"), lax.axis_size("ctx")
    length = ctx_count * rows
    scale = 1.0 / math.sqrt(seqs * length)
    first, last, twist, ahead, back = make_tables(ctx_count, rows)
    place = lax.axis_index("dp").astype(jnp.int32).reshape(1)
    taps = jnp.concatenate([short_filter, jnp.zeros((8 - tap_count, groups), F32)], axis=0)
    left_rim = neighbours(feats_in[rows - HALO :], 1)
    pair = (seqs, ctx_count, 2 * OWN, rows)
    wide_pad = pltpu.VMEM((rows + HALO, width_all), F32)
    wide_taps = pltpu.VMEM((8, width_all), F32)
    filt = call(
        functools.partial(filter_kernel, ctx_count),
        shape((OWN, ctx_count, 2 * rows), F32),
        [pltpu.VMEM((length // rows * OWN, rows), F32)],
        (place, long_filter, first, twist, ahead),
        (4e9, 2e6),
        1,
    )
    feats, sent = call(
        functools.partial(short_kernel, tap_count, group_size),
        (shape((rows, width_all), F32), shape(pair, BF16)),
        [wide_pad, wide_taps],
        (feats_in, left_rim, taps, cot),
        (4e9, 6e6),
    )
    got = lax.all_to_all(
        sent.reshape(seqs * ctx_count, 2 * OWN, rows), ("dp", "ctx"), 0, 0, tiled=True
    ).reshape(pair)
    long_rows = pltpu.VMEM((seqs * ctx_count * 2 * OWN, rows), F32)
    mixed, corr = call(
        functools.partial(mix_kernel, seqs, ctx_count),
        (shape(pair, BF16), shape((OWN, ctx_count, 2 * rows), F32)),
        [long_rows, long_rows],
        (got, filt, first, last, twist, ahead, back),
        (8e9, 6e6),
    )
    returned = lax.all_to_all(
        mixed.reshape(seqs * ctx_count, 2 * OWN, rows), ("dp", "ctx"), 0, 0, tiled=True
    ).reshape(pair)
    own_taps = call(
        functools.partial(taps_kernel, ctx_count, scale),
        shape((OWN, length), BF16),
        [pltpu.VMEM((ctx_count * OWN, rows), F32)],
        (corr, last, twist, back),
        (2e9, 1e6),
    )
    others = [partner(own_taps, "dp", mask) for mask in (1, 2, 3)]
    mixer_out, gso, edge, short_part = call(
        functools.partial(gate_kernel, tap_count, group_size, scale),
        (
            shape((rows, width), BF16),
            shape((rows, width_all), F32),
            shape((HALO, width_all), BF16),
            shape((8, groups), F32),
        ),
        [wide_pad, pltpu.VMEM((tap_count * 8, width_all), F32)],
        (returned, feats, cot, feats_in, left_rim),
        (4e9, 9e6),
    )
    right_rim = neighbours(edge, -1)
    grad_rows = call(
        functools.partial(back_kernel, tap_count, group_size),
        shape((rows, width_all), BF16),
        [pltpu.VMEM((rows + HALO, width_all), F32), wide_taps],
        (gso, right_rim, taps),
        (4e9, 6e6),
    )
    for axis in ("ctx", "dp"):
        mask = 1
        while mask < lax.axis_size(axis):
            short_part = short_part + partner(short_part, axis, mask)
            mask *= 2
    grad_long = call(
        join_kernel,
        shape((seqs * OWN, length), F32),
        [],
        (place, own_taps, *others),
        (1e8, 2e6),
        1,
    )
    return mixer_out[None], grad_rows[None], grad_long, short_part[:tap_count]


def solution(mesh):
    return jax.shard_map(
        shards,
        mesh=mesh,
        in_specs=(P("dp", "ctx", None), P(), P("ctx", None), P("dp", "ctx", None)),
        out_specs=(P("dp", "ctx", None), P("dp", "ctx", None), P("ctx", None), P()),
        check_vma=False,
    )
```

```python
import functools
import math

import jax
import jax.numpy as jnp
import numpy as np
from jax import lax
from jax.experimental import pallas as pl
from jax.experimental.pallas import tpu as pltpu
from jax.sharding import PartitionSpec as P

F32 = jnp.float32
BF16 = jnp.bfloat16
LANES = 128
OWN = 8
HALO = 8
ROT = -0.25
VMEM_LIMIT = 16 * 1024 * 1024


def two_parts(table):
    high = jnp.asarray(table, F32).astype(BF16)
    low = (jnp.asarray(table, F32) - high.astype(F32)).astype(BF16)
    return high, low


def make_tables(rows, cols):
    total = rows * cols
    k1 = np.arange(rows, dtype=np.float64)[:, None] + ROT
    n1 = np.arange(rows, dtype=np.float64)[None, :]
    turn = 2.0 * np.pi * k1 * n1 / rows
    first = np.concatenate([np.cos(turn), -np.sin(turn)], axis=0)
    last = np.concatenate([np.cos(turn.T), -np.sin(turn.T)], axis=1) / total
    n2 = np.arange(cols, dtype=np.float64)
    twist = 2.0 * np.pi * k1 * n2[None, :] / total
    twist = np.concatenate([np.cos(twist), -np.sin(twist)], axis=1)
    inner = 2.0 * np.pi * ((n2[:, None] * n2[None, :]) % cols) / cols
    real, imag = np.cos(inner), -np.sin(inner)
    ahead = np.block([[real, imag], [-imag, real]])
    back = np.block([[real, -imag], [imag, real]])
    first = jnp.concatenate(two_parts(first), axis=1)
    last = jnp.concatenate(two_parts(last), axis=1)
    ahead = jnp.concatenate(two_parts(ahead), axis=0)
    back = jnp.concatenate(two_parts(back), axis=0)
    return first, last, jnp.asarray(twist, F32), ahead, back


def mxu(left, right):
    return jnp.dot(left, right, preferred_element_type=F32)


def twice(array, axis):
    return jnp.concatenate([array, array], axis=axis)


def to_spectra(signals, first, twist, ahead):
    rows, cols = signals[0].shape
    wide = jnp.concatenate(signals, axis=1).astype(BF16)
    mixed = mxu(first, twice(wide, 0))
    twist_real, twist_imag = twist[:, :cols], twist[:, cols:]
    turned = []
    for at in range(len(signals)):
        real = mixed[:rows, at * cols : (at + 1) * cols]
        imag = mixed[rows:, at * cols : (at + 1) * cols]
        turned.append(
            jnp.concatenate(
                [real * twist_real - imag * twist_imag, real * twist_imag + imag * twist_real], axis=1
            )
        )
    turned = jnp.concatenate(turned, axis=0).astype(BF16)
    return mxu(twice(turned, 1), ahead)


def from_spectra(spectra, last, twist, back):
    rows, cols = spectra[0].shape[0], spectra[0].shape[1] // 2
    tall = jnp.concatenate(spectra, axis=0).astype(BF16)
    mixed = mxu(twice(tall, 1), back)
    twist_real, twist_imag = twist[:, :cols], twist[:, cols:]
    turned = []
    for at in range(len(spectra)):
        real = mixed[at * rows : (at + 1) * rows, :cols]
        imag = mixed[at * rows : (at + 1) * rows, cols:]
        turned.append(
            jnp.concatenate(
                [real * twist_real + imag * twist_imag, imag * twist_real - real * twist_imag], axis=0
            )
        )
    turned = jnp.concatenate(turned, axis=1).astype(BF16)
    return mxu(last, twice(turned, 0))


def times(left, right, flip):
    cols = left.shape[1] // 2
    left_real, left_imag = left[:, :cols], left[:, cols:]
    right_real, right_imag = right[:, :cols], right[:, cols:]
    if flip:
        real = left_real * right_real + left_imag * right_imag
        imag = left_imag * right_real - left_real * right_imag
    else:
        real = left_real * right_real - left_imag * right_imag
        imag = left_real * right_imag + left_imag * right_real
    return jnp.concatenate([real, imag], axis=1)


def filter_kernel(rows, place_ref, taps_ref, first_ref, twist_ref, ahead_ref, out_ref, spread):
    base = pl.multiple_of(place_ref[0] * OWN, OWN)
    for row in range(rows):
        spread[row * OWN : (row + 1) * OWN, :] = taps_ref[
            pl.ds(base, OWN), row * LANES : (row + 1) * LANES
        ]
    first, twist, ahead = first_ref[...], twist_ref[...], ahead_ref[...]
    twist_real, twist_imag = twist[:, :LANES], twist[:, LANES:]
    for half in range(2):
        wide = jnp.concatenate(
            [spread[pl.ds(half * 4 + at, rows, stride=OWN), :] for at in range(4)], axis=1
        )
        high = wide.astype(BF16)
        low = (wide - high.astype(F32)).astype(BF16)
        mixed = mxu(first, twice(high, 0)) + mxu(first[:, :rows], low)
        turned = []
        for at in range(4):
            real = mixed[:rows, at * LANES : (at + 1) * LANES]
            imag = mixed[rows:, at * LANES : (at + 1) * LANES]
            turned.append(
                jnp.concatenate(
                    [real * twist_real - imag * twist_imag, real * twist_imag + imag * twist_real],
                    axis=1,
                )
            )
        turned = jnp.concatenate(turned, axis=0)
        high = turned.astype(BF16)
        low = (turned - high.astype(F32)).astype(BF16)
        spectra = mxu(twice(high, 1), ahead) + mxu(low, ahead[: 2 * LANES])
        for at in range(4):
            out_ref[half * 4 + at] = spectra[at * rows : (at + 1) * rows]


def mix_kernel(
    seqs,
    rows,
    got_ref,
    filt_ref,
    first_ref,
    last_ref,
    twist_ref,
    ahead_ref,
    back_ref,
    out_ref,
    corr_ref,
    spread,
    gather,
):
    pair = 2 * OWN
    for seq in range(seqs):
        spread[seq * rows * pair : (seq + 1) * rows * pair, :] = (
            got_ref[seq].astype(F32).reshape(rows * pair, LANES)
        )
    first, last, twist = first_ref[...], last_ref[...], twist_ref[...]
    for chan in range(OWN):
        signals = [
            spread[pl.ds(seq * rows * pair + part * OWN + chan, rows, stride=pair), :]
            for part in range(2)
            for seq in range(seqs)
        ]
        spectra = to_spectra(signals, first, twist, ahead_ref[...])
        filt = filt_ref[chan]
        ahead_specs, back_specs, total = [], [], None
        for seq in range(seqs):
            prod = spectra[seq * rows : (seq + 1) * rows]
            grad = spectra[(seqs + seq) * rows : (seqs + seq + 1) * rows]
            ahead_specs.append(times(prod, filt, False))
            back_specs.append(times(grad, filt, True))
            term = times(grad, prod, True)
            total = term if total is None else total + term
        corr_ref[chan] = total
        result = from_spectra(ahead_specs + back_specs, last, twist, back_ref[...])
        at = 0
        for part in range(2):
            for seq in range(seqs):
                gather[pl.ds(seq * rows * pair + part * OWN + chan, rows, stride=pair), :] = result[
                    :, at * LANES : (at + 1) * LANES
                ]
                at += 1
    for seq in range(seqs):
        out_ref[seq] = (
            gather[seq * rows * pair : (seq + 1) * rows * pair, :]
            .reshape(rows, pair, LANES)
            .astype(BF16)
        )


def taps_kernel(rows, scale, corr_ref, last_ref, twist_ref, back_ref, out_ref, gather):
    last, twist, back = last_ref[...], twist_ref[...], back_ref[...]
    for half in range(2):
        result = from_spectra([corr_ref[half * 4 + at] for at in range(4)], last, twist, back)
        for at in range(4):
            gather[pl.ds(half * 4 + at, rows, stride=OWN), :] = (
                result[:, at * LANES : (at + 1) * LANES] * scale
            )
    for row in range(rows):
        out_ref[:, row * LANES : (row + 1) * LANES] = gather[row * OWN : (row + 1) * OWN, :].astype(BF16)


def join_kernel(place_ref, own_ref, one_ref, two_ref, three_ref, out_ref):
    place = place_ref[0]
    for step, ref in enumerate((own_ref, one_ref, two_ref, three_ref)):
        row = pl.multiple_of((place ^ step) * OWN, OWN)
        out_ref[pl.ds(row, OWN), :] = ref[...].astype(F32)


def group_table(groups, group_size):
    rows = lax.broadcasted_iota(jnp.int32, (groups, groups * group_size), 0)
    cols = lax.broadcasted_iota(jnp.int32, (groups, groups * group_size), 1)
    return jnp.where(cols // group_size == rows, 1.0, 0.0).astype(F32)


def spread_taps(taps_ref, group_size, wide):
    tap_count, groups = taps_ref.shape
    blocks = groups // LANES
    rows = jnp.concatenate(
        [
            jnp.concatenate([taps_ref[:, at * LANES : (at + 1) * LANES], jnp.zeros((8 - tap_count, LANES), F32)], axis=0)
            for at in range(blocks)
        ],
        axis=0,
    )
    high = rows.astype(BF16)
    rest = rows - high.astype(F32)
    middle = rest.astype(BF16)
    low = (rest - middle.astype(F32)).astype(BF16)
    table = group_table(LANES, group_size).astype(BF16)
    spread = mxu(high, table) + (mxu(middle, table) + mxu(low, table))
    for at in range(blocks):
        wide[:, at * LANES * group_size : (at + 1) * LANES * group_size] = spread[at * 8 : (at + 1) * 8]


def short_kernel(
    tap_count, group_size, qkv_ref, rim_ref, taps_ref, cot_ref, feats_ref, out_ref, wide, padded
):
    rows, width_all = qkv_ref.shape
    width = width_all // 3
    spread_taps(taps_ref, group_size, wide)
    padded[0:HALO, :] = rim_ref[...].astype(F32)
    padded[HALO : HALO + rows, :] = qkv_ref[...].astype(F32)
    per_chunk = LANES // OWN // 4

    def chunk(at, _):
        parts = []
        for part in range(3):
            cols = pl.ds(pl.multiple_of(part * width + at * LANES, LANES), LANES)
            total = wide[0:1, cols] * padded[HALO : HALO + rows, cols]
            for lag in range(1, tap_count):
                total = total + wide[lag : lag + 1, cols] * padded[HALO - lag : HALO - lag + rows, cols]
            feats_ref[:, cols] = total
            parts.append(total)
        cols = pl.ds(pl.multiple_of(at * LANES, LANES), LANES)
        product = (parts[1] * parts[2]).T.reshape(LANES // OWN, OWN, LANES)
        grad_in = (cot_ref[:, cols].astype(F32) * parts[0]).T.reshape(LANES // OWN, OWN, LANES)
        both = jnp.concatenate([product, grad_in], axis=1).astype(BF16)
        both = both.reshape(per_chunk, 4, 2 * OWN, LANES)
        for seq in range(4):
            out_ref[seq, pl.ds(at * per_chunk, per_chunk)] = both[:, seq]
        return 0

    lax.fori_loop(0, width // LANES, chunk, 0)


def gate_kernel(
    tap_count,
    group_size,
    scale,
    got_ref,
    feats_ref,
    cot_ref,
    qkv_ref,
    rim_ref,
    mixer_ref,
    gso_ref,
    edge_ref,
    short_ref,
    padded,
    sums,
):
    rows, width_all = qkv_ref.shape
    width = width_all // 3
    padded[0:HALO, :] = rim_ref[...].astype(F32)
    padded[HALO : HALO + rows, :] = qkv_ref[...].astype(F32)
    per_chunk = LANES // OWN // 4

    def chunk(at, _):
        both = jnp.stack(
            [got_ref[seq, pl.ds(at * per_chunk, per_chunk)] for seq in range(4)], axis=1
        ).astype(F32)
        both = both.reshape(LANES // OWN, 2 * OWN, LANES)
        long_out = both[:, :OWN].reshape(LANES, LANES).T
        grad_product = both[:, OWN:].reshape(LANES, LANES).T
        cols = [
            pl.ds(pl.multiple_of(part * width + at * LANES, LANES), LANES) for part in range(3)
        ]
        mixer_ref[:, cols[0]] = (feats_ref[:, cols[0]] * long_out).astype(BF16)
        grads = (
            cot_ref[:, cols[0]].astype(F32) * long_out,
            grad_product * feats_ref[:, cols[2]],
            grad_product * feats_ref[:, cols[1]],
        )
        for part in range(3):
            gso_ref[:, cols[part]] = grads[part]
            edge_ref[:, cols[part]] = grads[part][:HALO].astype(BF16)
            for lag in range(tap_count):
                term = grads[part] * padded[HALO - lag : HALO - lag + rows, cols[part]]
                sums[lag * 8 : (lag + 1) * 8, cols[part]] = jnp.sum(
                    term.reshape(rows // 8, 8, LANES), axis=0
                )
        return 0

    lax.fori_loop(0, width // LANES, chunk, 0)
    table = group_table(LANES, group_size)
    block = LANES * group_size
    for at in range(width_all // block):
        lags = [
            jnp.sum(sums[lag * 8 : (lag + 1) * 8, at * block : (at + 1) * block], axis=0, keepdims=True)
            for lag in range(tap_count)
        ]
        lags = jnp.concatenate(lags + [jnp.zeros((8 - tap_count, block), F32)], axis=0)
        short_ref[:, at * LANES : (at + 1) * LANES] = (
            lax.dot_general(
                lags,
                table,
                (((1,), (1,)), ((), ())),
                precision=lax.Precision.HIGHEST,
                preferred_element_type=F32,
            )
            * scale
        )


def back_kernel(tap_count, gso_ref, rim_ref, wide, out_ref, padded):
    rows, width_all = gso_ref.shape
    padded[rows - HALO : rows, :] = gso_ref[rows - HALO : rows, :]
    padded[rows : rows + HALO, :] = rim_ref[...].astype(F32)
    body = rows - HALO

    def chunk(at, _):
        cols = pl.ds(pl.multiple_of(at * LANES, LANES), LANES)
        total = wide[0:1, cols] * gso_ref[0:body, cols]
        tail = wide[0:1, cols] * padded[body:rows, cols]
        for lag in range(1, tap_count):
            total = total + wide[lag : lag + 1, cols] * gso_ref[lag : lag + body, cols]
            tail = tail + wide[lag : lag + 1, cols] * padded[body + lag : rows + lag, cols]
        out_ref[:, cols] = jnp.concatenate([total, tail], axis=0).astype(BF16)
        return 0

    lax.fori_loop(0, width_all // LANES, chunk, 0)


def call(kernel, outs, scratch, args, cost, scalars=0):
    vmem = pl.BlockSpec(memory_space=pltpu.VMEM)
    smem = pl.BlockSpec(memory_space=pltpu.SMEM)
    flops, moved = (int(value) for value in cost)
    return pl.pallas_call(
        kernel,
        out_shape=outs,
        in_specs=[smem] * scalars + [vmem] * (len(args) - scalars),
        out_specs=jax.tree.map(lambda _: vmem, outs),
        scratch_shapes=scratch,
        compiler_params=pltpu.CompilerParams(vmem_limit_bytes=VMEM_LIMIT),
        cost_estimate=pl.CostEstimate(flops=flops, bytes_accessed=moved, transcendentals=0),
    )(*args)


def shape(dims, kind):
    return jax.ShapeDtypeStruct(dims, kind)


def neighbours(array, by):
    devices = lax.axis_size("ctx")
    pairs = [(i, i + by) for i in range(devices) if 0 <= i + by < devices]
    return lax.ppermute(array, "ctx", pairs)


def partner(array, axis, mask):
    return lax.ppermute(array, axis, [(i, i ^ mask) for i in range(lax.axis_size(axis))])


def shards(qkv, short_filter, long_filter, cotangent):
    feats_in, cot = qkv[0], cotangent[0]
    rows, width_all = feats_in.shape
    width = width_all // 3
    tap_count, groups = short_filter.shape
    group_size = width_all // groups
    seqs, ctx_count = lax.axis_size("dp"), lax.axis_size("ctx")
    length = ctx_count * rows
    scale = 1.0 / math.sqrt(seqs * length)
    first, last, twist, ahead, back = make_tables(ctx_count, rows)
    place = lax.axis_index("dp").astype(jnp.int32).reshape(1)
    left_rim = neighbours(feats_in[rows - HALO :], 1)
    pair = (seqs, ctx_count, 2 * OWN, rows)
    wide_pad = pltpu.VMEM((rows + HALO, width_all), F32)
    filt = call(
        functools.partial(filter_kernel, ctx_count),
        shape((OWN, ctx_count, 2 * rows), F32),
        [pltpu.VMEM((length // rows * OWN, rows), F32)],
        (place, long_filter, first, twist, ahead),
        (4e9, 2e6),
        1,
    )
    feats, sent, wide_taps = call(
        functools.partial(short_kernel, tap_count, group_size),
        (shape((rows, width_all), F32), shape(pair, BF16), shape((8, width_all), F32)),
        [wide_pad],
        (feats_in, left_rim, short_filter, cot),
        (4e9, 6e6),
    )
    got = lax.all_to_all(
        sent.reshape(seqs * ctx_count, 2 * OWN, rows), ("dp", "ctx"), 0, 0, tiled=True
    ).reshape(pair)
    long_rows = pltpu.VMEM((seqs * ctx_count * 2 * OWN, rows), F32)
    mixed, corr = call(
        functools.partial(mix_kernel, seqs, ctx_count),
        (shape(pair, BF16), shape((OWN, ctx_count, 2 * rows), F32)),
        [long_rows, long_rows],
        (got, filt, first, last, twist, ahead, back),
        (8e9, 6e6),
    )
    returned = lax.all_to_all(
        mixed.reshape(seqs * ctx_count, 2 * OWN, rows), ("dp", "ctx"), 0, 0, tiled=True
    ).reshape(pair)
    own_taps = call(
        functools.partial(taps_kernel, ctx_count, scale),
        shape((OWN, length), BF16),
        [pltpu.VMEM((ctx_count * OWN, rows), F32)],
        (corr, last, twist, back),
        (2e9, 1e6),
    )
    others = [partner(own_taps, "dp", mask) for mask in (1, 2, 3)]
    grad_long = call(
        join_kernel,
        shape((seqs * OWN, length), F32),
        [],
        (place, own_taps, *others),
        (1e8, 2e6),
        1,
    )
    returned, grad_long = lax.optimization_barrier((returned, grad_long))
    mixer_out, gso, edge, short_part = call(
        functools.partial(gate_kernel, tap_count, group_size, scale),
        (
            shape((rows, width), BF16),
            shape((rows, width_all), F32),
            shape((HALO, width_all), BF16),
            shape((8, groups), F32),
        ),
        [wide_pad, pltpu.VMEM((tap_count * 8, width_all), F32)],
        (returned, feats, cot, feats_in, left_rim),
        (4e9, 9e6),
    )
    right_rim = neighbours(edge, -1)
    masks = [(axis, 1 << bit) for axis in ("ctx", "dp") for bit in range((lax.axis_size(axis) - 1).bit_length())]
    for axis, mask in masks:
        if (axis, mask) == ("ctx", ctx_count // 2):
            gso, right_rim, short_part = lax.optimization_barrier((gso, right_rim, short_part))
            grad_rows = call(
                functools.partial(back_kernel, tap_count),
                shape((rows, width_all), BF16),
                [wide_pad],
                (gso, right_rim, wide_taps),
                (4e9, 6e6),
            )
        short_part = short_part + partner(short_part, axis, mask)
        if (axis, mask) == ("ctx", ctx_count // 2):
            grad_rows, short_part = lax.optimization_barrier((grad_rows, short_part))
    return mixer_out[None], grad_rows[None], grad_long, short_part[:tap_count]


def solution(mesh):
    return jax.shard_map(
        shards,
        mesh=mesh,
        in_specs=(P("dp", "ctx", None), P(), P("ctx", None), P("dp", "ctx", None)),
        out_specs=(P("dp", "ctx", None), P("dp", "ctx", None), P("ctx", None), P()),
        check_vma=False,
    )
```

```python
import functools
import math

import jax
import jax.numpy as jnp
import numpy as np
from jax import lax
from jax.experimental import pallas as pl
from jax.experimental.pallas import tpu as pltpu
from jax.sharding import PartitionSpec as P

F32 = jnp.float32
BF16 = jnp.bfloat16
LANES = 128
OWN = 8
TAPS = 7
HALO = 8
ROT = -0.25
GRANT = 16 * 1024 * 1024
BLOCK = 512


def two_parts(table):
    high = jnp.asarray(table, F32).astype(BF16)
    low = (jnp.asarray(table, F32) - high.astype(F32)).astype(BF16)
    return high, low


def make_tables(rows, cols):
    total = rows * cols
    k1 = np.arange(rows, dtype=np.float64)[:, None] + ROT
    n1 = np.arange(rows, dtype=np.float64)[None, :]
    turn = 2.0 * np.pi * k1 * n1 / rows
    first = np.concatenate([np.cos(turn), -np.sin(turn)], axis=0)
    last = np.concatenate([np.cos(turn.T), -np.sin(turn.T)], axis=1) / total
    n2 = np.arange(cols, dtype=np.float64)
    twist = 2.0 * np.pi * k1 * n2[None, :] / total
    twist = np.concatenate([np.cos(twist), -np.sin(twist)], axis=1)
    inner = 2.0 * np.pi * ((n2[:, None] * n2[None, :]) % cols) / cols
    real, imag = np.cos(inner), -np.sin(inner)
    ahead = np.block([[real, imag], [-imag, real]])
    back = np.block([[real, -imag], [imag, real]])
    first = jnp.concatenate(two_parts(first), axis=1)
    last = jnp.concatenate(two_parts(last), axis=1)
    ahead = jnp.concatenate(two_parts(ahead), axis=0)
    back = jnp.concatenate(two_parts(back), axis=0)
    return first, last, jnp.asarray(twist, F32), ahead, back


def mxu(left, right):
    return jnp.dot(left, right, preferred_element_type=F32)


def twice(array, axis):
    return jnp.concatenate([array, array], axis=axis)


def to_spectra(signals, first, twist, ahead):
    rows, cols = signals[0].shape
    wide = jnp.concatenate(signals, axis=1).astype(BF16)
    mixed = mxu(first, twice(wide, 0))
    twist_real, twist_imag = twist[:, :cols], twist[:, cols:]
    turned = []
    for at in range(len(signals)):
        real = mixed[:rows, at * cols : (at + 1) * cols]
        imag = mixed[rows:, at * cols : (at + 1) * cols]
        turned.append(
            jnp.concatenate(
                [real * twist_real - imag * twist_imag, real * twist_imag + imag * twist_real], axis=1
            )
        )
    turned = jnp.concatenate(turned, axis=0).astype(BF16)
    return mxu(twice(turned, 1), ahead)


def from_spectra(spectra, last, twist, back):
    rows, cols = spectra[0].shape[0], spectra[0].shape[1] // 2
    tall = jnp.concatenate(spectra, axis=0).astype(BF16)
    mixed = mxu(twice(tall, 1), back)
    twist_real, twist_imag = twist[:, :cols], twist[:, cols:]
    turned = []
    for at in range(len(spectra)):
        real = mixed[at * rows : (at + 1) * rows, :cols]
        imag = mixed[at * rows : (at + 1) * rows, cols:]
        turned.append(
            jnp.concatenate(
                [real * twist_real + imag * twist_imag, imag * twist_real - real * twist_imag], axis=0
            )
        )
    turned = jnp.concatenate(turned, axis=1).astype(BF16)
    return mxu(last, twice(turned, 0))


def times(left, right, flip):
    cols = left.shape[1] // 2
    left_real, left_imag = left[:, :cols], left[:, cols:]
    right_real, right_imag = right[:, :cols], right[:, cols:]
    if flip:
        real = left_real * right_real + left_imag * right_imag
        imag = left_imag * right_real - left_real * right_imag
    else:
        real = left_real * right_real - left_imag * right_imag
        imag = left_real * right_imag + left_imag * right_real
    return jnp.concatenate([real, imag], axis=1)


def filter_spectra(rows, base, taps_ref, first, twist, ahead, out_ref, spread):
    for row in range(rows):
        spread[row * OWN : (row + 1) * OWN, :] = taps_ref[
            pl.ds(base, OWN), row * LANES : (row + 1) * LANES
        ]
    twist_real, twist_imag = twist[:, :LANES], twist[:, LANES:]
    for half in range(2):
        wide = jnp.concatenate(
            [spread[pl.ds(half * 4 + at, rows, stride=OWN), :] for at in range(4)], axis=1
        )
        high = wide.astype(BF16)
        low = (wide - high.astype(F32)).astype(BF16)
        mixed = mxu(first, twice(high, 0)) + mxu(first[:, :rows], low)
        turned = []
        for at in range(4):
            real = mixed[:rows, at * LANES : (at + 1) * LANES]
            imag = mixed[rows:, at * LANES : (at + 1) * LANES]
            turned.append(
                jnp.concatenate(
                    [real * twist_real - imag * twist_imag, real * twist_imag + imag * twist_real],
                    axis=1,
                )
            )
        turned = jnp.concatenate(turned, axis=0)
        high = turned.astype(BF16)
        low = (turned - high.astype(F32)).astype(BF16)
        spectra = mxu(twice(high, 1), ahead) + mxu(low, ahead[: 2 * LANES])
        for at in range(4):
            out_ref[half * 4 + at] = spectra[at * rows : (at + 1) * rows]


def mix_kernel(
    seqs,
    rows,
    place_ref,
    got_ref,
    taps_ref,
    first_ref,
    last_ref,
    twist_ref,
    ahead_ref,
    back_ref,
    out_ref,
    corr_ref,
    spread,
    gather,
    filt_ref,
):
    pair = 2 * OWN
    filter_spectra(
        rows,
        pl.multiple_of(place_ref[0] * OWN, OWN),
        taps_ref,
        first_ref[...],
        twist_ref[...],
        ahead_ref[...],
        filt_ref,
        gather,
    )
    for seq in range(seqs):
        spread[seq * rows * pair : (seq + 1) * rows * pair, :] = (
            got_ref[seq].astype(F32).reshape(rows * pair, LANES)
        )
    first, last, twist = first_ref[...], last_ref[...], twist_ref[...]
    for chan in range(OWN):
        signals = [
            spread[pl.ds(seq * rows * pair + part * OWN + chan, rows, stride=pair), :]
            for part in range(2)
            for seq in range(seqs)
        ]
        spectra = to_spectra(signals, first, twist, ahead_ref[...])
        filt = filt_ref[chan]
        ahead_specs, back_specs, total = [], [], None
        for seq in range(seqs):
            prod = spectra[seq * rows : (seq + 1) * rows]
            grad = spectra[(seqs + seq) * rows : (seqs + seq + 1) * rows]
            ahead_specs.append(times(prod, filt, False))
            back_specs.append(times(grad, filt, True))
            term = times(grad, prod, True)
            total = term if total is None else total + term
        corr_ref[chan] = total
        result = from_spectra(ahead_specs + back_specs, last, twist, back_ref[...])
        at = 0
        for part in range(2):
            for seq in range(seqs):
                gather[pl.ds(seq * rows * pair + part * OWN + chan, rows, stride=pair), :] = result[
                    :, at * LANES : (at + 1) * LANES
                ]
                at += 1
    for seq in range(seqs):
        out_ref[seq] = (
            gather[seq * rows * pair : (seq + 1) * rows * pair, :]
            .reshape(rows, pair, LANES)
            .astype(BF16)
        )


def taps_kernel(rows, scale, corr_ref, last_ref, twist_ref, back_ref, out_ref, gather):
    last, twist, back = last_ref[...], twist_ref[...], back_ref[...]
    for half in range(2):
        result = from_spectra([corr_ref[half * 4 + at] for at in range(4)], last, twist, back)
        for at in range(4):
            gather[pl.ds(half * 4 + at, rows, stride=OWN), :] = (
                result[:, at * LANES : (at + 1) * LANES] * scale
            )
    for row in range(rows):
        out_ref[:, row * LANES : (row + 1) * LANES] = gather[row * OWN : (row + 1) * OWN, :].astype(BF16)


def join_kernel(place_ref, own_ref, one_ref, two_ref, three_ref, out_ref):
    place = place_ref[0]
    for step, ref in enumerate((own_ref, one_ref, two_ref, three_ref)):
        row = pl.multiple_of((place ^ step) * OWN, OWN)
        out_ref[pl.ds(row, OWN), :] = ref[...].astype(F32)


def group_table(groups, group_size):
    rows = lax.broadcasted_iota(jnp.int32, (groups, groups * group_size), 0)
    cols = lax.broadcasted_iota(jnp.int32, (groups, groups * group_size), 1)
    return jnp.where(cols // group_size == rows, 1.0, 0.0).astype(F32)


def spread_taps(taps_ref, group_size, wide):
    tap_count, groups = taps_ref.shape
    blocks = groups // LANES
    rows = jnp.concatenate(
        [
            jnp.concatenate([taps_ref[:, at * LANES : (at + 1) * LANES], jnp.zeros((8 - tap_count, LANES), F32)], axis=0)
            for at in range(blocks)
        ],
        axis=0,
    )
    high = rows.astype(BF16)
    rest = rows - high.astype(F32)
    middle = rest.astype(BF16)
    low = (rest - middle.astype(F32)).astype(BF16)
    table = group_table(LANES, group_size).astype(BF16)
    spread = mxu(high, table) + (mxu(middle, table) + mxu(low, table))
    for at in range(blocks):
        wide[:, at * LANES * group_size : (at + 1) * LANES * group_size] = spread[at * 8 : (at + 1) * 8]


def short_rows(padded, wide, cols, first_row, rows):
    start = first_row + HALO
    total = wide(0) * padded[start : start + rows, cols]
    for lag in range(1, TAPS):
        total = total + wide(lag) * padded[start - lag : start - lag + rows, cols]
    return total


def owner_tiles(product, grad_in):
    tiles = [array.reshape(LANES // OWN, OWN, LANES) for array in (product, grad_in)]
    return jnp.concatenate(tiles, axis=1).astype(BF16).reshape(LANES // OWN // 4, 4, 2 * OWN, LANES)


def short_kernel(
    group_size, width, q_ref, k_ref, v_ref, cot_ref, taps_ref, feats_ref, out_ref, wide_ref, padded
):
    step = pl.program_id(0)
    rows, block = q_ref.shape

    @pl.when(step == 0)
    def _():
        spread_taps(taps_ref, group_size, wide_ref)
        padded[0:HALO, :] = jnp.zeros((HALO, 3 * block), F32)

    for part, ref in enumerate((q_ref, k_ref, v_ref)):
        padded[HALO : HALO + rows, part * block : (part + 1) * block] = ref[...].astype(F32)
    per_chunk = LANES // OWN // 4
    for at in range(block // LANES):
        here = slice(at * LANES, (at + 1) * LANES)
        parts = []
        for part in range(3):
            lanes = pl.ds(pl.multiple_of(part * width + step * block + at * LANES, LANES), LANES)
            cols = slice(part * block + at * LANES, part * block + (at + 1) * LANES)
            total = short_rows(padded, lambda lag: wide_ref[lag : lag + 1, lanes], cols, 0, rows)
            feats_ref[part, :, here] = total
            parts.append(total)
        tiles = owner_tiles((parts[1] * parts[2]).T, (cot_ref[:, here].astype(F32) * parts[0]).T)
        for seq in range(4):
            out_ref[seq, at * per_chunk : (at + 1) * per_chunk] = tiles[:, seq]


def rim_kernel(width, top_ref, rim_ref, cot_ref, wide_ref, feats_in, sent_in, feats_ref, out_ref, padded):
    padded[0:HALO, :] = rim_ref[...].astype(F32)
    padded[HALO : 2 * HALO, :] = top_ref[...].astype(F32)[:HALO]
    per_chunk = LANES // OWN // 4
    fresh = lax.broadcasted_iota(jnp.int32, (per_chunk, 2 * OWN, LANES), 2) < HALO
    blank = jnp.zeros((LANES - HALO, LANES), F32)
    for at in range(width // LANES):
        parts = []
        for part in range(3):
            cols = slice(part * width + at * LANES, part * width + (at + 1) * LANES)
            total = short_rows(padded, lambda lag: wide_ref[lag : lag + 1, cols], cols, 0, HALO)
            feats_ref[part, :, at * LANES : (at + 1) * LANES] = total
            parts.append(total)
        cot = cot_ref[:, at * LANES : (at + 1) * LANES].astype(F32)[:HALO]
        product = jnp.concatenate([parts[1] * parts[2], blank], axis=0).T
        grad_in = jnp.concatenate([cot * parts[0], blank], axis=0).T
        tiles = owner_tiles(product, grad_in)
        here = slice(at * per_chunk, (at + 1) * per_chunk)
        for seq in range(4):
            out_ref[seq, here] = jnp.where(fresh, tiles[:, seq], sent_in[seq, here])


def gate_kernel(
    group_size,
    scale,
    got_ref,
    feats_ref,
    cot_ref,
    qkv_ref,
    rim_ref,
    mixer_ref,
    gso_ref,
    edge_ref,
    short_ref,
    padded,
    sums,
):
    rows, width_all = qkv_ref.shape
    width = width_all // 3
    padded[0:HALO, :] = rim_ref[...].astype(F32)
    padded[HALO : HALO + rows, :] = qkv_ref[...].astype(F32)
    per_chunk = LANES // OWN // 4

    def chunk(at, _):
        here = pl.ds(pl.multiple_of(at * LANES, LANES), LANES)
        both = jnp.stack(
            [got_ref[seq, pl.ds(at * per_chunk, per_chunk)] for seq in range(4)], axis=1
        ).astype(F32)
        both = both.reshape(LANES // OWN, 2 * OWN, LANES)
        long_out = both[:, :OWN].reshape(LANES, LANES).T
        grad_product = both[:, OWN:].reshape(LANES, LANES).T
        mixer_ref[:, here] = (feats_ref[0, :, here] * long_out).astype(BF16)
        grads = (
            cot_ref[:, here].astype(F32) * long_out,
            grad_product * feats_ref[2, :, here],
            grad_product * feats_ref[1, :, here],
        )
        for part in range(3):
            cols = pl.ds(pl.multiple_of(part * width + at * LANES, LANES), LANES)
            gso_ref[:, cols] = grads[part]
            edge_ref[:, cols] = grads[part][:HALO].astype(BF16)
            for lag in range(TAPS):
                term = grads[part] * padded[HALO - lag : HALO - lag + rows, cols]
                sums[lag * 8 : (lag + 1) * 8, cols] = jnp.sum(
                    term.reshape(rows // 8, 8, LANES), axis=0
                )
        return 0

    lax.fori_loop(0, width // LANES, chunk, 0)
    span = LANES * group_size
    blocks = width_all // span
    lags = []
    for at in range(blocks):
        lags += [
            jnp.sum(sums[lag * 8 : (lag + 1) * 8, at * span : (at + 1) * span], axis=0, keepdims=True)
            for lag in range(TAPS)
        ]
        lags.append(jnp.zeros((8 - TAPS, span), F32))
    lags = jnp.concatenate(lags, axis=0)
    high = lags.astype(BF16)
    rest = lags - high.astype(F32)
    middle = rest.astype(BF16)
    low = (rest - middle.astype(F32)).astype(BF16)
    table = group_table(LANES, group_size).astype(BF16)
    dims = (((1,), (1,)), ((), ()))
    total = lax.dot_general(
        jnp.concatenate([high, middle, low], axis=0), table, dims, preferred_element_type=F32
    )
    count = blocks * 8
    total = total[:count] + (total[count : 2 * count] + total[2 * count :])
    for at in range(blocks):
        short_ref[:, at * LANES : (at + 1) * LANES] = total[at * 8 : (at + 1) * 8] * scale


def back_kernel(gso_ref, rim_ref, wide_ref, out_ref, tail):
    rows, width_all = gso_ref.shape
    body = rows - HALO
    tail[0:HALO, :] = gso_ref[body:rows, :]
    tail[HALO : 2 * HALO, :] = rim_ref[...].astype(F32)

    def chunk(at, _):
        cols = pl.ds(pl.multiple_of(at * LANES, LANES), LANES)
        total = wide_ref[0:1, cols] * gso_ref[0:body, cols]
        end = wide_ref[0:1, cols] * tail[0:HALO, cols]
        for lag in range(1, TAPS):
            total = total + wide_ref[lag : lag + 1, cols] * gso_ref[lag : lag + body, cols]
            end = end + wide_ref[lag : lag + 1, cols] * tail[lag : lag + HALO, cols]
        out_ref[:, cols] = jnp.concatenate([total, end], axis=0).astype(BF16)
        return 0

    lax.fori_loop(0, width_all // LANES, chunk, 0)


def call(kernel, outs, scratch, args, cost, scalars=0):
    vmem = pl.BlockSpec(memory_space=pltpu.VMEM)
    smem = pl.BlockSpec(memory_space=pltpu.SMEM)
    return pl.pallas_call(
        kernel,
        out_shape=outs,
        in_specs=[smem] * scalars + [vmem] * (len(args) - scalars),
        out_specs=jax.tree.map(lambda _: vmem, outs),
        scratch_shapes=scratch,
        compiler_params=pltpu.CompilerParams(vmem_limit_bytes=GRANT),
        cost_estimate=estimate(*cost),
    )(*args)


def estimate(flops, moved):
    return pl.CostEstimate(flops=int(flops), bytes_accessed=int(moved), transcendentals=0)


def grid_call(kernel, steps, outs, out_specs, scratch, args, in_specs, cost, aliases=None):
    return pl.pallas_call(
        kernel,
        grid=(steps,),
        out_shape=outs,
        in_specs=in_specs,
        out_specs=out_specs,
        scratch_shapes=scratch,
        input_output_aliases=aliases or {},
        compiler_params=pltpu.CompilerParams(vmem_limit_bytes=GRANT),
        cost_estimate=estimate(*cost),
    )(*args)


def shape(dims, kind):
    return jax.ShapeDtypeStruct(dims, kind)


def neighbours(array, by):
    devices = lax.axis_size("ctx")
    pairs = [(i, i + by) for i in range(devices) if 0 <= i + by < devices]
    return lax.ppermute(array, "ctx", pairs)


def partner(array, axis, mask):
    return lax.ppermute(array, axis, [(i, i ^ mask) for i in range(lax.axis_size(axis))])


def shards(qkv, short_filter, long_filter, cotangent):
    feats_in, cot = qkv[0], cotangent[0]
    rows, width_all = feats_in.shape
    width = width_all // 3
    tap_count, groups = short_filter.shape
    group_size = width_all // groups
    seqs, ctx_count = lax.axis_size("dp"), lax.axis_size("ctx")
    length = ctx_count * rows
    scale = 1.0 / math.sqrt(seqs * length)
    first, last, twist, ahead, back = make_tables(ctx_count, rows)
    place = lax.axis_index("dp").astype(jnp.int32).reshape(1)
    left_rim = neighbours(feats_in[rows - HALO :], 1)
    pair = (seqs, ctx_count, 2 * OWN, rows)
    block = BLOCK
    steps = width // block
    owners = block // OWN // seqs
    lanes = [
        pl.BlockSpec((rows, block), lambda i, part=part: (0, part * steps + i)) for part in range(3)
    ]
    triple = pl.BlockSpec((3, rows, block), lambda i: (0, 0, i))
    tiles = pl.BlockSpec((seqs, owners, 2 * OWN, rows), lambda i: (0, i, 0, 0))
    padded = pltpu.VMEM((rows + HALO, 3 * block), F32)
    whole = lambda *dims: pl.BlockSpec(dims, lambda i: (0,) * len(dims))
    feats_shape = shape((3, rows, width), F32)
    feats, sent, wide_taps = grid_call(
        functools.partial(short_kernel, group_size, width),
        steps,
        (feats_shape, shape(pair, BF16), shape((8, width_all), F32)),
        (triple, tiles, whole(8, width_all)),
        [padded],
        (feats_in, feats_in, feats_in, cot, short_filter),
        [*lanes, lanes[0], whole(tap_count, groups)],
        (1e9, 6e6),
    )
    top = pl.BlockSpec((2 * HALO, width_all), lambda i: (0, 0))
    rows_top = pl.BlockSpec((3, HALO, width), lambda i: (0, 0, 0))
    feats, sent = grid_call(
        functools.partial(rim_kernel, width),
        1,
        (feats_shape, shape(pair, BF16)),
        (rows_top, whole(*pair)),
        [pltpu.VMEM((2 * HALO, width_all), F32)],
        (feats_in, left_rim, cot, wide_taps, feats, sent),
        [
            top,
            whole(HALO, width_all),
            pl.BlockSpec((2 * HALO, width), lambda i: (0, 0)),
            whole(8, width_all),
            rows_top,
            whole(*pair),
        ],
        (1e8, 2e6),
        {4: 0, 5: 1},
    )
    got = lax.all_to_all(
        sent.reshape(seqs * ctx_count, 2 * OWN, rows), ("dp", "ctx"), 0, 0, tiled=True
    ).reshape(pair)
    long_rows = pltpu.VMEM((seqs * ctx_count * 2 * OWN, rows), F32)
    spectra = (OWN, ctx_count, 2 * rows)
    mixed, corr = call(
        functools.partial(mix_kernel, seqs, ctx_count),
        (shape(pair, BF16), shape(spectra, F32)),
        [long_rows, long_rows, pltpu.VMEM(spectra, F32)],
        (place, got, long_filter, first, last, twist, ahead, back),
        (8e9, 6e6),
        1,
    )
    returned = lax.all_to_all(
        mixed.reshape(seqs * ctx_count, 2 * OWN, rows), ("dp", "ctx"), 0, 0, tiled=True
    ).reshape(pair)
    own_taps = call(
        functools.partial(taps_kernel, ctx_count, scale),
        shape((OWN, length), BF16),
        [pltpu.VMEM((ctx_count * OWN, rows), F32)],
        (corr, last, twist, back),
        (1e9, 1e6),
    )
    returned, own_taps = lax.optimization_barrier((returned, own_taps))
    mixer_out, gso, edge, short_part = call(
        functools.partial(gate_kernel, group_size, scale),
        (
            shape((rows, width), BF16),
            shape((rows, width_all), F32),
            shape((HALO, width_all), BF16),
            shape((8, groups), F32),
        ),
        [pltpu.VMEM((rows + HALO, width_all), F32), pltpu.VMEM((tap_count * 8, width_all), F32)],
        (returned, feats, cot, feats_in, left_rim),
        (1e9, 9e6),
    )
    right_rim = neighbours(edge, -1)
    masks = [
        (axis, 1 << bit)
        for axis in ("ctx", "dp")
        for bit in range((lax.axis_size(axis) - 1).bit_length())
    ]
    for at, (axis, mask) in enumerate(masks):
        if at == 2:
            own_taps, short_part = lax.optimization_barrier((own_taps, short_part))
            others = [partner(own_taps, "dp", step) for step in (1, 2, 3)]
        if at == 5:
            gso, right_rim, short_part = lax.optimization_barrier((gso, right_rim, short_part))
            grad_rows = call(
                back_kernel,
                shape((rows, width_all), BF16),
                [pltpu.VMEM((2 * HALO, width_all), F32)],
                (gso, right_rim, wide_taps),
                (1e9, 6e6),
            )
        if at == 7:
            others, short_part = lax.optimization_barrier((others, short_part))
            grad_long = call(
                join_kernel,
                shape((seqs * OWN, length), F32),
                [],
                (place, own_taps, *others),
                (1e8, 2e6),
                1,
            )
        short_part = short_part + partner(short_part, axis, mask)
        if at == 5:
            grad_rows, short_part = lax.optimization_barrier((grad_rows, short_part))
    return mixer_out[None], grad_rows[None], grad_long, short_part[:tap_count]


def solution(mesh):
    return jax.shard_map(
        shards,
        mesh=mesh,
        in_specs=(P("dp", "ctx", None), P(), P("ctx", None), P("dp", "ctx", None)),
        out_specs=(P("dp", "ctx", None), P("dp", "ctx", None), P("ctx", None), P()),
        check_vma=False,
    )
```

```python
import functools
import math

import jax
import jax.numpy as jnp
import numpy as np
from jax import lax
from jax.experimental import pallas as pl
from jax.experimental.pallas import tpu as pltpu
from jax.sharding import PartitionSpec as P

F32 = jnp.float32
BF16 = jnp.bfloat16
LANES = 128
OWN = 8
TAPS = 7
HALO = 8
ROT = -0.25
GRANT = 16 * 1024 * 1024
FIRST_GRANT = 16 * 1024 * 1024
BLOCK = 512


def two_parts(table):
    high = jnp.asarray(table, F32).astype(BF16)
    low = (jnp.asarray(table, F32) - high.astype(F32)).astype(BF16)
    return high, low


def make_tables(rows, cols):
    total = rows * cols
    k1 = np.arange(rows, dtype=np.float64)[:, None] + ROT
    n1 = np.arange(rows, dtype=np.float64)[None, :]
    turn = 2.0 * np.pi * k1 * n1 / rows
    first = np.concatenate([np.cos(turn), -np.sin(turn)], axis=0)
    last = np.concatenate([np.cos(turn.T), -np.sin(turn.T)], axis=1) / total
    n2 = np.arange(cols, dtype=np.float64)
    twist = 2.0 * np.pi * k1 * n2[None, :] / total
    twist = np.concatenate([np.cos(twist), -np.sin(twist)], axis=1)
    inner = 2.0 * np.pi * ((n2[:, None] * n2[None, :]) % cols) / cols
    real, imag = np.cos(inner), -np.sin(inner)
    ahead = np.block([[real, imag], [-imag, real]])
    back = np.block([[real, -imag], [imag, real]])
    first = jnp.concatenate(two_parts(first), axis=1)
    last = jnp.concatenate(two_parts(last), axis=1)
    ahead = jnp.concatenate(two_parts(ahead), axis=0)
    back = jnp.concatenate(two_parts(back), axis=0)
    return first, last, jnp.asarray(twist, F32), ahead, back


def mxu(left, right):
    return jnp.dot(left, right, preferred_element_type=F32)


def twice(array, axis):
    return jnp.concatenate([array, array], axis=axis)


def to_spectra(signals, first, twist, ahead):
    rows, cols = signals[0].shape
    wide = jnp.concatenate(signals, axis=1).astype(BF16)
    mixed = mxu(first[:, :rows], wide)
    twist_real, twist_imag = twist[:, :cols], twist[:, cols:]
    turned = []
    for at in range(len(signals)):
        real = mixed[:rows, at * cols : (at + 1) * cols]
        imag = mixed[rows:, at * cols : (at + 1) * cols]
        turned.append(
            jnp.concatenate(
                [real * twist_real - imag * twist_imag, real * twist_imag + imag * twist_real], axis=1
            )
        )
    turned = jnp.concatenate(turned, axis=0).astype(BF16)
    return mxu(turned, ahead[: 2 * cols])


def from_spectra(spectra, last, twist, back):
    rows, cols = spectra[0].shape[0], spectra[0].shape[1] // 2
    tall = jnp.concatenate(spectra, axis=0).astype(BF16)
    mixed = mxu(tall, back[: 2 * cols])
    twist_real, twist_imag = twist[:, :cols], twist[:, cols:]
    turned = []
    for at in range(len(spectra)):
        real = mixed[at * rows : (at + 1) * rows, :cols]
        imag = mixed[at * rows : (at + 1) * rows, cols:]
        turned.append(
            jnp.concatenate(
                [real * twist_real + imag * twist_imag, imag * twist_real - real * twist_imag], axis=0
            )
        )
    turned = jnp.concatenate(turned, axis=1).astype(BF16)
    return mxu(last[:, : 2 * rows], turned)


def times(left, right, flip):
    cols = left.shape[1] // 2
    left_real, left_imag = left[:, :cols], left[:, cols:]
    right_real, right_imag = right[:, :cols], right[:, cols:]
    if flip:
        real = left_real * right_real + left_imag * right_imag
        imag = left_imag * right_real - left_real * right_imag
    else:
        real = left_real * right_real - left_imag * right_imag
        imag = left_real * right_imag + left_imag * right_real
    return jnp.concatenate([real, imag], axis=1)


def filter_spectra(rows, base, taps_ref, first, twist, ahead, out_ref, spread):
    for row in range(rows):
        spread[row * OWN : (row + 1) * OWN, :] = taps_ref[
            pl.ds(base, OWN), row * LANES : (row + 1) * LANES
        ]
    twist_real, twist_imag = twist[:, :LANES], twist[:, LANES:]
    for half in range(2):
        wide = jnp.concatenate(
            [spread[pl.ds(half * 4 + at, rows, stride=OWN), :] for at in range(4)], axis=1
        )
        high = wide.astype(BF16)
        low = (wide - high.astype(F32)).astype(BF16)
        mixed = mxu(first, twice(high, 0)) + mxu(first[:, :rows], low)
        turned = []
        for at in range(4):
            real = mixed[:rows, at * LANES : (at + 1) * LANES]
            imag = mixed[rows:, at * LANES : (at + 1) * LANES]
            turned.append(
                jnp.concatenate(
                    [real * twist_real - imag * twist_imag, real * twist_imag + imag * twist_real],
                    axis=1,
                )
            )
        turned = jnp.concatenate(turned, axis=0)
        high = turned.astype(BF16)
        low = (turned - high.astype(F32)).astype(BF16)
        spectra = mxu(twice(high, 1), ahead) + mxu(low, ahead[: 2 * LANES])
        for at in range(4):
            out_ref[half * 4 + at] = spectra[at * rows : (at + 1) * rows]


def mix_kernel(
    seqs,
    rows,
    scale,
    place_ref,
    got_ref,
    taps_ref,
    first_ref,
    last_ref,
    twist_ref,
    ahead_ref,
    back_ref,
    out_ref,
    grad_ref,
    spread,
    gather,
    filt_ref,
    corr_ref,
):
    pair = 2 * OWN
    filter_spectra(
        rows,
        pl.multiple_of(place_ref[0] * OWN, OWN),
        taps_ref,
        first_ref[...],
        twist_ref[...],
        ahead_ref[...],
        filt_ref,
        gather,
    )
    for seq in range(seqs):
        spread[seq * rows * pair : (seq + 1) * rows * pair, :] = (
            got_ref[seq].astype(F32).reshape(rows * pair, LANES)
        )
    first, last, twist = first_ref[...], last_ref[...], twist_ref[...]
    for chan in range(OWN):
        signals = [
            spread[pl.ds(seq * rows * pair + part * OWN + chan, rows, stride=pair), :]
            for part in range(2)
            for seq in range(seqs)
        ]
        spectra = to_spectra(signals, first, twist, ahead_ref[...])
        filt = filt_ref[chan]
        ahead_specs, back_specs, total = [], [], None
        for seq in range(seqs):
            prod = spectra[seq * rows : (seq + 1) * rows]
            grad = spectra[(seqs + seq) * rows : (seqs + seq + 1) * rows]
            ahead_specs.append(times(prod, filt, False))
            back_specs.append(times(grad, filt, True))
            term = times(grad, prod, True)
            total = term if total is None else total + term
        corr_ref[chan] = total
        result = from_spectra(ahead_specs + back_specs, last, twist, back_ref[...])
        at = 0
        for part in range(2):
            for seq in range(seqs):
                gather[pl.ds(seq * rows * pair + part * OWN + chan, rows, stride=pair), :] = result[
                    :, at * LANES : (at + 1) * LANES
                ]
                at += 1
    for seq in range(seqs):
        out_ref[seq] = (
            gather[seq * rows * pair : (seq + 1) * rows * pair, :]
            .reshape(rows, pair, LANES)
            .astype(BF16)
        )
    for half in range(2):
        result = from_spectra([corr_ref[half * 4 + at] for at in range(4)], last, twist, back_ref[...])
        for at in range(4):
            spread[pl.ds(half * 4 + at, rows, stride=OWN), :] = (
                result[:, at * LANES : (at + 1) * LANES] * scale
            )
    for row in range(rows):
        grad_ref[:, row * LANES : (row + 1) * LANES] = spread[row * OWN : (row + 1) * OWN, :].astype(
            BF16
        )


def join_kernel(place_ref, own_ref, one_ref, two_ref, three_ref, out_ref):
    place = place_ref[0]
    for step, ref in enumerate((own_ref, one_ref, two_ref, three_ref)):
        row = pl.multiple_of((place ^ step) * OWN, OWN)
        out_ref[pl.ds(row, OWN), :] = ref[...].astype(F32)


def group_table(groups, group_size):
    rows = lax.broadcasted_iota(jnp.int32, (groups, groups * group_size), 0)
    cols = lax.broadcasted_iota(jnp.int32, (groups, groups * group_size), 1)
    return jnp.where(cols // group_size == rows, 1.0, 0.0).astype(F32)


def spread_taps(taps_ref, group_size, wide):
    tap_count, groups = taps_ref.shape
    blocks = groups // LANES
    rows = jnp.concatenate(
        [
            jnp.concatenate([taps_ref[:, at * LANES : (at + 1) * LANES], jnp.zeros((8 - tap_count, LANES), F32)], axis=0)
            for at in range(blocks)
        ],
        axis=0,
    )
    high = rows.astype(BF16)
    rest = rows - high.astype(F32)
    middle = rest.astype(BF16)
    low = (rest - middle.astype(F32)).astype(BF16)
    table = group_table(LANES, group_size).astype(BF16)
    spread = mxu(high, table) + (mxu(middle, table) + mxu(low, table))
    for at in range(blocks):
        wide[:, at * LANES * group_size : (at + 1) * LANES * group_size] = spread[at * 8 : (at + 1) * 8]


def short_rows(padded, wide, cols, first_row, rows):
    start = first_row + HALO
    total = wide(0) * padded[start : start + rows, cols]
    for lag in range(1, TAPS):
        total = total + wide(lag) * padded[start - lag : start - lag + rows, cols]
    return total


def owner_tiles(product, grad_in):
    tiles = [array.reshape(LANES // OWN, OWN, LANES) for array in (product, grad_in)]
    return jnp.concatenate(tiles, axis=1).astype(BF16).reshape(LANES // OWN // 4, 4, 2 * OWN, LANES)


def short_kernel(
    group_size,
    taps_hbm,
    qkv_hbm,
    cot_hbm,
    feats_ref,
    out_ref,
    wide_ref,
    taps_ref,
    qkv_ref,
    cot_ref,
    padded,
    sems,
):
    rows, width_all = qkv_ref.shape
    width = width_all // 3
    steps = width // BLOCK
    copies = [(taps_hbm, taps_ref)]
    for step in range(steps):
        for part in range(3):
            cols = pl.ds(part * width + step * BLOCK, BLOCK)
            copies.append((qkv_hbm.at[:, cols], qkv_ref.at[:, cols]))
        cols = pl.ds(step * BLOCK, BLOCK)
        copies.append((cot_hbm.at[:, cols], cot_ref.at[:, cols]))
    copies = [
        pltpu.make_async_copy(source, target, sems.at[at]) for at, (source, target) in enumerate(copies)
    ]
    for copy in copies:
        copy.start()
    copies[0].wait()
    spread_taps(taps_ref, group_size, wide_ref)
    padded[0:HALO, :] = jnp.zeros((HALO, width_all), F32)
    per_chunk = LANES // OWN // 4
    per_step = BLOCK // LANES
    for at in range(width // LANES):
        if at % per_step == 0:
            for copy in copies[at // per_step * 4 + 1 : at // per_step * 4 + 5]:
                copy.wait()
        here = slice(at * LANES, (at + 1) * LANES)
        parts = []
        for part in range(3):
            cols = slice(part * width + at * LANES, part * width + (at + 1) * LANES)
            padded[HALO : HALO + rows, cols] = qkv_ref[:, cols].astype(F32)
            total = short_rows(padded, lambda lag: wide_ref[lag : lag + 1, cols], cols, 0, rows)
            feats_ref[part, :, here] = total
            parts.append(total)
        tiles = owner_tiles((parts[1] * parts[2]).T, (cot_ref[:, here].astype(F32) * parts[0]).T)
        for seq in range(4):
            out_ref[seq, at * per_chunk : (at + 1) * per_chunk] = tiles[:, seq]


def rim_kernel(width, top_ref, rim_ref, cot_ref, wide_ref, feats_in, sent_in, feats_ref, out_ref, padded):
    padded[0:HALO, :] = rim_ref[...].astype(F32)
    padded[HALO : 2 * HALO, :] = top_ref[...].astype(F32)[:HALO]
    per_chunk = LANES // OWN // 4
    fresh = lax.broadcasted_iota(jnp.int32, (per_chunk, 2 * OWN, LANES), 2) < HALO
    blank = jnp.zeros((LANES - HALO, LANES), F32)
    for at in range(width // LANES):
        parts = []
        for part in range(3):
            cols = slice(part * width + at * LANES, part * width + (at + 1) * LANES)
            total = short_rows(padded, lambda lag: wide_ref[lag : lag + 1, cols], cols, 0, HALO)
            feats_ref[part, :, at * LANES : (at + 1) * LANES] = total
            parts.append(total)
        cot = cot_ref[:, at * LANES : (at + 1) * LANES].astype(F32)[:HALO]
        product = jnp.concatenate([parts[1] * parts[2], blank], axis=0).T
        grad_in = jnp.concatenate([cot * parts[0], blank], axis=0).T
        tiles = owner_tiles(product, grad_in)
        here = slice(at * per_chunk, (at + 1) * per_chunk)
        for seq in range(4):
            out_ref[seq, here] = jnp.where(fresh, tiles[:, seq], sent_in[seq, here])


def gate_kernel(
    group_size,
    scale,
    got_ref,
    feats_ref,
    cot_ref,
    qkv_ref,
    rim_ref,
    mixer_ref,
    gso_ref,
    edge_ref,
    short_ref,
    padded,
    sums,
):
    rows, width_all = qkv_ref.shape
    width = width_all // 3
    padded[0:HALO, :] = rim_ref[...].astype(F32)
    padded[HALO : HALO + rows, :] = qkv_ref[...].astype(F32)
    per_chunk = LANES // OWN // 4

    def chunk(at, _):
        here = pl.ds(pl.multiple_of(at * LANES, LANES), LANES)
        both = jnp.stack(
            [got_ref[seq, pl.ds(at * per_chunk, per_chunk)] for seq in range(4)], axis=1
        ).astype(F32)
        both = both.reshape(LANES // OWN, 2 * OWN, LANES)
        long_out = both[:, :OWN].reshape(LANES, LANES).T
        grad_product = both[:, OWN:].reshape(LANES, LANES).T
        mixer_ref[:, here] = (feats_ref[0, :, here] * long_out).astype(BF16)
        grads = (
            cot_ref[:, here].astype(F32) * long_out,
            grad_product * feats_ref[2, :, here],
            grad_product * feats_ref[1, :, here],
        )
        for part in range(3):
            cols = pl.ds(pl.multiple_of(part * width + at * LANES, LANES), LANES)
            gso_ref[:, cols] = grads[part]
            edge_ref[:, cols] = grads[part][:HALO].astype(BF16)
            for lag in range(TAPS):
                term = grads[part] * padded[HALO - lag : HALO - lag + rows, cols]
                sums[lag * 8 : (lag + 1) * 8, cols] = jnp.sum(
                    term.reshape(rows // 8, 8, LANES), axis=0
                )
        return 0

    lax.fori_loop(0, width // LANES, chunk, 0)
    span = LANES * group_size
    blocks = width_all // span
    lags = []
    for at in range(blocks):
        lags += [
            jnp.sum(sums[lag * 8 : (lag + 1) * 8, at * span : (at + 1) * span], axis=0, keepdims=True)
            for lag in range(TAPS)
        ]
        lags.append(jnp.zeros((8 - TAPS, span), F32))
    lags = jnp.concatenate(lags, axis=0)
    high = lags.astype(BF16)
    rest = lags - high.astype(F32)
    middle = rest.astype(BF16)
    low = (rest - middle.astype(F32)).astype(BF16)
    table = group_table(LANES, group_size).astype(BF16)
    dims = (((1,), (1,)), ((), ()))
    total = lax.dot_general(
        jnp.concatenate([high, middle, low], axis=0), table, dims, preferred_element_type=F32
    )
    count = blocks * 8
    total = total[:count] + (total[count : 2 * count] + total[2 * count :])
    for at in range(blocks):
        short_ref[:, at * LANES : (at + 1) * LANES] = total[at * 8 : (at + 1) * 8] * scale


def back_kernel(gso_ref, rim_ref, wide_ref, out_ref, tail):
    rows, width_all = gso_ref.shape
    body = rows - HALO
    tail[0:HALO, :] = gso_ref[body:rows, :]
    tail[HALO : 2 * HALO, :] = rim_ref[...].astype(F32)

    def chunk(at, _):
        cols = pl.ds(pl.multiple_of(at * LANES, LANES), LANES)
        total = wide_ref[0:1, cols] * gso_ref[0:body, cols]
        end = wide_ref[0:1, cols] * tail[0:HALO, cols]
        for lag in range(1, TAPS):
            total = total + wide_ref[lag : lag + 1, cols] * gso_ref[lag : lag + body, cols]
            end = end + wide_ref[lag : lag + 1, cols] * tail[lag : lag + HALO, cols]
        out_ref[:, cols] = jnp.concatenate([total, end], axis=0).astype(BF16)
        return 0

    lax.fori_loop(0, width_all // LANES, chunk, 0)


def call(kernel, outs, scratch, args, cost, scalars=0):
    vmem = pl.BlockSpec(memory_space=pltpu.VMEM)
    smem = pl.BlockSpec(memory_space=pltpu.SMEM)
    return pl.pallas_call(
        kernel,
        out_shape=outs,
        in_specs=[smem] * scalars + [vmem] * (len(args) - scalars),
        out_specs=jax.tree.map(lambda _: vmem, outs),
        scratch_shapes=scratch,
        compiler_params=pltpu.CompilerParams(vmem_limit_bytes=GRANT),
        cost_estimate=estimate(*cost),
    )(*args)


def estimate(flops, moved):
    return pl.CostEstimate(flops=int(flops), bytes_accessed=int(moved), transcendentals=0)


def grid_call(kernel, steps, outs, out_specs, scratch, args, in_specs, cost, limit, aliases=None):
    return pl.pallas_call(
        kernel,
        grid=(steps,),
        out_shape=outs,
        in_specs=in_specs,
        out_specs=out_specs,
        scratch_shapes=scratch,
        input_output_aliases=aliases or {},
        compiler_params=pltpu.CompilerParams(vmem_limit_bytes=limit),
        cost_estimate=estimate(*cost),
    )(*args)


def shape(dims, kind):
    return jax.ShapeDtypeStruct(dims, kind)


def neighbours(array, by):
    devices = lax.axis_size("ctx")
    pairs = [(i, i + by) for i in range(devices) if 0 <= i + by < devices]
    return lax.ppermute(array, "ctx", pairs)


def partner(array, axis, mask):
    devices = lax.axis_size(axis)
    return lax.ppermute(array, axis, [(i, i ^ mask) for i in range(devices)])


def shards(qkv, short_filter, long_filter, cotangent):
    feats_in, cot = qkv[0], cotangent[0]
    rows, width_all = feats_in.shape
    width = width_all // 3
    tap_count, groups = short_filter.shape
    group_size = width_all // groups
    seqs, ctx_count = lax.axis_size("dp"), lax.axis_size("ctx")
    length = ctx_count * rows
    scale = 1.0 / math.sqrt(seqs * length)
    first, last, twist, ahead, back = make_tables(ctx_count, rows)
    place = lax.axis_index("dp").astype(jnp.int32).reshape(1)
    left_rim = neighbours(feats_in[rows - HALO :], 1)
    pair = (seqs, ctx_count, 2 * OWN, rows)
    vmem = pl.BlockSpec(memory_space=pltpu.VMEM)
    whole = lambda *dims: pl.BlockSpec(dims, lambda i: (0,) * len(dims))
    feats_shape = shape((3, rows, width), F32)
    hbm = pl.BlockSpec(memory_space=pltpu.HBM)
    feats, sent, wide_taps = grid_call(
        functools.partial(short_kernel, group_size),
        1,
        (feats_shape, shape(pair, BF16), shape((8, width_all), F32)),
        (vmem, vmem, vmem),
        [
            pltpu.VMEM((tap_count, groups), F32),
            pltpu.VMEM((rows, width_all), BF16),
            pltpu.VMEM((rows, width), BF16),
            pltpu.VMEM((rows + HALO, width_all), F32),
            pltpu.SemaphoreType.DMA((4 * width // BLOCK + 1,)),
        ],
        [pltpu.with_memory_space_constraint(arg, pltpu.HBM) for arg in (short_filter, feats_in, cot)],
        [hbm, hbm, hbm],
        (1e9, 6e6),
        FIRST_GRANT,
    )
    top = pl.BlockSpec((2 * HALO, width_all), lambda i: (0, 0))
    rows_top = pl.BlockSpec((3, HALO, width), lambda i: (0, 0, 0))
    feats, sent = grid_call(
        functools.partial(rim_kernel, width),
        1,
        (feats_shape, shape(pair, BF16)),
        (rows_top, whole(*pair)),
        [pltpu.VMEM((2 * HALO, width_all), F32)],
        (feats_in, left_rim, cot, wide_taps, feats, sent),
        [
            top,
            whole(HALO, width_all),
            pl.BlockSpec((2 * HALO, width), lambda i: (0, 0)),
            whole(8, width_all),
            rows_top,
            whole(*pair),
        ],
        (1e8, 2e6),
        GRANT,
        {4: 0, 5: 1},
    )
    sent, place = lax.optimization_barrier((sent, place))
    got = lax.all_to_all(
        sent.reshape(seqs * ctx_count, 2 * OWN, rows), ("dp", "ctx"), 0, 0, tiled=True
    ).reshape(pair)
    long_rows = pltpu.VMEM((seqs * ctx_count * 2 * OWN, rows), F32)
    spectra = (OWN, ctx_count, 2 * rows)
    mixed, own_taps = call(
        functools.partial(mix_kernel, seqs, ctx_count, scale),
        (shape(pair, BF16), shape((OWN, length), BF16)),
        [long_rows, long_rows, pltpu.VMEM(spectra, F32), pltpu.VMEM(spectra, F32)],
        (place, got, long_filter, first, last, twist, ahead, back),
        (8e9, 6e6),
        1,
    )
    returned = lax.all_to_all(
        mixed.reshape(seqs * ctx_count, 2 * OWN, rows), ("dp", "ctx"), 0, 0, tiled=True
    ).reshape(pair)
    mixer_out, gso, edge, short_part = call(
        functools.partial(gate_kernel, group_size, scale),
        (
            shape((rows, width), BF16),
            shape((rows, width_all), F32),
            shape((HALO, width_all), BF16),
            shape((8, groups), F32),
        ),
        [pltpu.VMEM((rows + HALO, width_all), F32), pltpu.VMEM((tap_count * 8, width_all), F32)],
        (returned, feats, cot, feats_in, left_rim),
        (1e9, 9e6),
    )
    right_rim = neighbours(edge, -1)
    far = ctx_count // 2
    hops = [("ctx", 1), ("ctx", 2), ("ctx", 6), ("ctx", 8), ("ctx", 24)]
    hops += [(("dp", "ctx"), (seqs - 1) * ctx_count + far), ("dp", 1), ("dp", 2)]
    for at, (axis, mask) in enumerate(hops):
        if at == 2:
            own_taps, short_part = lax.optimization_barrier((own_taps, short_part))
            others = [partner(own_taps, "dp", step) for step in (1, 2, 3)]
        if at == 5:
            gso, right_rim, short_part = lax.optimization_barrier((gso, right_rim, short_part))
            grad_rows = call(
                back_kernel,
                shape((rows, width_all), BF16),
                [pltpu.VMEM((2 * HALO, width_all), F32)],
                (gso, right_rim, wide_taps),
                (1e9, 6e6),
            )
        if at == 7:
            others, short_part = lax.optimization_barrier((others, short_part))
            grad_long = call(
                join_kernel,
                shape((seqs * OWN, length), F32),
                [],
                (place, own_taps, *others),
                (1e8, 2e6),
                1,
            )
        short_part = short_part + partner(short_part, axis, mask)
        if at == 5:
            grad_rows, short_part = lax.optimization_barrier((grad_rows, short_part))
    return mixer_out[None], grad_rows[None], grad_long, short_part[:tap_count]


def solution(mesh):
    return jax.shard_map(
        shards,
        mesh=mesh,
        in_specs=(P("dp", "ctx", None), P(), P("ctx", None), P("dp", "ctx", None)),
        out_specs=(P("dp", "ctx", None), P("dp", "ctx", None), P("ctx", None), P()),
        check_vma=False,
    )
```

```python
import functools
import math

import jax
import jax.numpy as jnp
import numpy as np
from jax import lax
from jax.experimental import pallas as pl
from jax.experimental.pallas import tpu as pltpu
from jax.sharding import PartitionSpec as P

F32 = jnp.float32
BF16 = jnp.bfloat16
LANES = 128
OWN = 8
TAPS = 7
HALO = 8
ROT = -0.25
GRANT = 16 * 1024 * 1024
FIRST_GRANT = 16 * 1024 * 1024
BLOCK = 1024


def two_parts(table):
    high = jnp.asarray(table, F32).astype(BF16)
    low = (jnp.asarray(table, F32) - high.astype(F32)).astype(BF16)
    return high, low


def phase_order(rows):
    place = np.arange(rows)
    return (place % 8) * (rows // 8) + place // 8


def make_tables(rows, cols):
    total = rows * cols
    k1 = np.arange(rows, dtype=np.float64)[:, None] + ROT
    n1 = np.arange(rows, dtype=np.float64)[None, :]
    turn = 2.0 * np.pi * k1 * n1 / rows
    first = np.concatenate([np.cos(turn), -np.sin(turn)], axis=0)
    last = np.concatenate([np.cos(turn.T), -np.sin(turn.T)], axis=1) / total
    n2 = np.arange(cols, dtype=np.float64)
    twist = 2.0 * np.pi * k1 * n2[None, :] / total
    inner = 2.0 * np.pi * ((n2[:, None] * n2[None, :]) % cols) / cols
    real, imag = np.cos(inner), -np.sin(inner)
    order = phase_order(cols)
    high, low = two_parts(np.block([[real, imag], [-imag, real]]))
    back = np.block([[real, -imag], [imag, real]])
    ahead_phases = np.block([[real[order], imag[order]], [-imag[order], real[order]]])
    back_phases = np.block([[real[:, order], -imag[:, order]], [imag[:, order], real[:, order]]])
    outer = jnp.concatenate([jnp.concatenate(two_parts(first), axis=1), two_parts(last)[0]], axis=0)
    inner = [high, low] + [two_parts(table)[0] for table in (back, ahead_phases, back_phases)]
    twists = [np.cos(twist), -np.sin(twist), np.cos(twist[:, order]), -np.sin(twist[:, order])]
    return outer, jnp.concatenate(inner, axis=0), jnp.asarray(np.concatenate(twists, axis=1), F32)


def mxu(left, right):
    return jnp.dot(left, right, preferred_element_type=F32)


def twice(array, axis):
    return jnp.concatenate([array, array], axis=axis)


def to_spectra(signals, first, twist, ahead):
    rows, cols = signals[0].shape
    wide = jnp.concatenate(signals, axis=1).astype(BF16)
    mixed = mxu(first, wide)
    twist_real, twist_imag = twist[:, :cols], twist[:, cols:]
    turned = []
    for at in range(len(signals)):
        real = mixed[:rows, at * cols : (at + 1) * cols]
        imag = mixed[rows:, at * cols : (at + 1) * cols]
        turned.append(
            jnp.concatenate(
                [real * twist_real - imag * twist_imag, real * twist_imag + imag * twist_real], axis=1
            )
        )
    turned = jnp.concatenate(turned, axis=0).astype(BF16)
    return mxu(turned, ahead)


def from_spectra(spectra, last, twist, back):
    rows, cols = spectra[0].shape[0], spectra[0].shape[1] // 2
    tall = jnp.concatenate(spectra, axis=0).astype(BF16)
    mixed = mxu(tall, back)
    twist_real, twist_imag = twist[:, :cols], twist[:, cols:]
    turned = []
    for at in range(len(spectra)):
        real = mixed[at * rows : (at + 1) * rows, :cols]
        imag = mixed[at * rows : (at + 1) * rows, cols:]
        turned.append(
            jnp.concatenate(
                [real * twist_real + imag * twist_imag, imag * twist_real - real * twist_imag], axis=0
            )
        )
    turned = jnp.concatenate(turned, axis=1).astype(BF16)
    return mxu(last, turned)


def times(left, right, flip):
    cols = left.shape[1] // 2
    left_real, left_imag = left[:, :cols], left[:, cols:]
    right_real, right_imag = right[:, :cols], right[:, cols:]
    if flip:
        real = left_real * right_real + left_imag * right_imag
        imag = left_imag * right_real - left_real * right_imag
    else:
        real = left_real * right_real - left_imag * right_imag
        imag = left_real * right_imag + left_imag * right_real
    return jnp.concatenate([real, imag], axis=1)


def filter_spectra(rows, base, taps_ref, first, twist, ahead, out_ref, spread):
    for row in range(rows):
        spread[row * OWN : (row + 1) * OWN, :] = taps_ref[
            pl.ds(base, OWN), row * LANES : (row + 1) * LANES
        ]
    twist_real, twist_imag = twist[:, :LANES], twist[:, LANES:]
    for half in range(2):
        wide = jnp.concatenate(
            [spread[pl.ds(half * 4 + at, rows, stride=OWN), :] for at in range(4)], axis=1
        )
        high = wide.astype(BF16)
        low = (wide - high.astype(F32)).astype(BF16)
        mixed = mxu(first, twice(high, 0)) + mxu(first[:, :rows], low)
        turned = []
        for at in range(4):
            real = mixed[:rows, at * LANES : (at + 1) * LANES]
            imag = mixed[rows:, at * LANES : (at + 1) * LANES]
            turned.append(
                jnp.concatenate(
                    [real * twist_real - imag * twist_imag, real * twist_imag + imag * twist_real],
                    axis=1,
                )
            )
        turned = jnp.concatenate(turned, axis=0)
        high = turned.astype(BF16)
        low = (turned - high.astype(F32)).astype(BF16)
        spectra = mxu(twice(high, 1), ahead) + mxu(low, ahead[: 2 * LANES])
        for at in range(4):
            out_ref[half * 4 + at] = spectra[at * rows : (at + 1) * rows]


def mix_kernel(
    seqs,
    rows,
    scale,
    place_ref,
    got_ref,
    taps_ref,
    outer_ref,
    inner_ref,
    twist_ref,
    out_ref,
    grad_ref,
    spread,
    gather,
    filt_ref,
    corr_ref,
):
    pair = 2 * OWN
    side = 2 * LANES
    filter_spectra(
        rows,
        pl.multiple_of(place_ref[0] * OWN, OWN),
        taps_ref,
        outer_ref[: 2 * rows],
        twist_ref[:, :side],
        inner_ref[: 2 * side],
        filt_ref,
        gather,
    )
    for seq in range(seqs):
        spread[seq * rows * pair : (seq + 1) * rows * pair, :] = (
            got_ref[seq].astype(F32).reshape(rows * pair, LANES)
        )
    first, last = outer_ref[: 2 * rows, :rows], outer_ref[2 * rows :]
    back = inner_ref[2 * side : 3 * side]
    ahead_phases, back_phases = inner_ref[3 * side : 4 * side], inner_ref[4 * side :]
    twist, twist_phases = twist_ref[:, :side], twist_ref[:, side:]
    for chan in range(OWN):
        signals = [
            spread[pl.ds(seq * rows * pair + part * OWN + chan, rows, stride=pair), :]
            for part in range(2)
            for seq in range(seqs)
        ]
        spectra = to_spectra(signals, first, twist_phases, ahead_phases)
        filt = filt_ref[chan]
        ahead_specs, back_specs, total = [], [], None
        for seq in range(seqs):
            prod = spectra[seq * rows : (seq + 1) * rows]
            grad = spectra[(seqs + seq) * rows : (seqs + seq + 1) * rows]
            ahead_specs.append(times(prod, filt, False))
            back_specs.append(times(grad, filt, True))
            term = times(grad, prod, True)
            total = term if total is None else total + term
        corr_ref[chan] = total
        result = from_spectra(ahead_specs + back_specs, last, twist_phases, back_phases)
        at = 0
        for part in range(2):
            for seq in range(seqs):
                gather[pl.ds(seq * rows * pair + part * OWN + chan, rows, stride=pair), :] = result[
                    :, at * LANES : (at + 1) * LANES
                ]
                at += 1
    for seq in range(seqs):
        out_ref[seq] = (
            gather[seq * rows * pair : (seq + 1) * rows * pair, :]
            .reshape(rows, pair, LANES)
            .astype(BF16)
        )
    for half in range(2):
        result = from_spectra([corr_ref[half * 4 + at] for at in range(4)], last, twist, back)
        for at in range(4):
            spread[pl.ds(half * 4 + at, rows, stride=OWN), :] = (
                result[:, at * LANES : (at + 1) * LANES] * scale
            )
    for row in range(rows):
        grad_ref[:, row * LANES : (row + 1) * LANES] = spread[row * OWN : (row + 1) * OWN, :].astype(
            BF16
        )


def join_kernel(place_ref, own_ref, one_ref, two_ref, three_ref, out_ref):
    place = place_ref[0]
    for step, ref in enumerate((own_ref, one_ref, two_ref, three_ref)):
        row = pl.multiple_of((place ^ step) * OWN, OWN)
        out_ref[pl.ds(row, OWN), :] = ref[...].astype(F32)


def group_table(groups, group_size):
    rows = lax.broadcasted_iota(jnp.int32, (groups, groups * group_size), 0)
    cols = lax.broadcasted_iota(jnp.int32, (groups, groups * group_size), 1)
    return jnp.where(cols // group_size == rows, 1.0, 0.0).astype(F32)


def spread_taps(taps_ref, group_size, wide):
    tap_count, groups = taps_ref.shape
    blocks = groups // LANES
    rows = jnp.concatenate(
        [
            jnp.concatenate([taps_ref[:, at * LANES : (at + 1) * LANES], jnp.zeros((8 - tap_count, LANES), F32)], axis=0)
            for at in range(blocks)
        ],
        axis=0,
    )
    high = rows.astype(BF16)
    rest = rows - high.astype(F32)
    middle = rest.astype(BF16)
    low = (rest - middle.astype(F32)).astype(BF16)
    table = group_table(LANES, group_size).astype(BF16)
    spread = mxu(high, table) + (mxu(middle, table) + mxu(low, table))
    for at in range(blocks):
        wide[:, at * LANES * group_size : (at + 1) * LANES * group_size] = spread[at * 8 : (at + 1) * 8]


def phased(stage, first, count):
    reach = (stage.shape[0] - HALO) // 8
    return jnp.concatenate(
        [stage[pl.ds(HALO + first + at, 8, stride=reach), :] for at in range(count)], axis=0
    )


def unphased(stage, array):
    reach = array.shape[0] // 8
    for at in range(reach):
        stage[pl.ds(at, 8, stride=reach), :] = array[at * 8 : (at + 1) * 8]
    return stage[...]


def owner_tiles(product, grad_in):
    tiles = [array.reshape(LANES // OWN, OWN, LANES) for array in (product, grad_in)]
    return jnp.concatenate(tiles, axis=1).astype(BF16).reshape(LANES // OWN // 4, 4, 2 * OWN, LANES)


def short_kernel(
    group_size,
    taps_hbm,
    qkv_hbm,
    cot_hbm,
    feats_ref,
    out_ref,
    wide_ref,
    taps_ref,
    qkv_ref,
    cot_ref,
    stages,
    sems,
):
    rows, width_all = qkv_ref.shape
    width = width_all // 3
    steps = width // BLOCK
    copies = [(taps_hbm, taps_ref)]
    for step in range(steps):
        for part in range(3):
            cols = pl.ds(part * width + step * BLOCK, BLOCK)
            copies.append((qkv_hbm.at[:, cols], qkv_ref.at[:, cols]))
        cols = pl.ds(step * BLOCK, BLOCK)
        copies.append((cot_hbm.at[:, cols], cot_ref.at[:, cols]))
    copies = [
        pltpu.make_async_copy(source, target, sems.at[at]) for at, (source, target) in enumerate(copies)
    ]
    for copy in copies:
        copy.start()
    copies[0].wait()
    spread_taps(taps_ref, group_size, wide_ref)
    for at in range(8):
        stages[at, 0:HALO, :] = jnp.zeros((HALO, LANES), F32)
    per_chunk = LANES // OWN // 4
    per_step = BLOCK // LANES
    for at in range(width // LANES):
        if at % per_step == 0:
            for copy in copies[at // per_step * 4 + 1 : at // per_step * 4 + 5]:
                copy.wait()
        parts = []
        for part in range(3):
            stage = stages.at[at % 2 * 4 + part]
            cols = slice(part * width + at * LANES, part * width + (at + 1) * LANES)
            stage[HALO:, :] = qkv_ref[:, cols].astype(F32)
            shifted = phased(stage, 1 - TAPS, rows // 8 + TAPS - 1)
            total = wide_ref[0:1, cols] * shifted[(TAPS - 1) * 8 :]
            for lag in range(1, TAPS):
                start = (TAPS - 1 - lag) * 8
                total = total + wide_ref[lag : lag + 1, cols] * shifted[start : start + rows]
            feats_ref[part * (width // LANES) + at] = total
            parts.append(total)
        stage = stages.at[at % 2 * 4 + 3]
        stage[HALO:, :] = cot_ref[:, at * LANES : (at + 1) * LANES].astype(F32)
        cot = phased(stage, 0, rows // 8)
        tiles = owner_tiles((parts[1] * parts[2]).T, (cot * parts[0]).T)
        for seq in range(4):
            out_ref[seq, at * per_chunk : (at + 1) * per_chunk] = tiles[:, seq]


def rim_kernel(
    width, top_ref, rim_ref, cot_ref, wide_ref, feats_in, sent_in, feats_ref, out_ref, padded, first_rows
):
    padded[0:HALO, :] = rim_ref[...].astype(F32)
    padded[HALO : 2 * HALO, :] = top_ref[...].astype(F32)[:HALO]
    per_chunk = LANES // OWN // 4
    chunks = width // LANES
    lane = lax.broadcasted_iota(jnp.int32, (per_chunk, 2 * OWN, LANES), 2)
    fresh = (lane % 8 == 0) & (lane < 8 * HALO)
    fresh_rows = lax.broadcasted_iota(jnp.int32, (8 * HALO, LANES), 0) % 8 == 0
    for at in range(chunks):
        parts = []
        for part in range(3):
            cols = slice(part * width + at * LANES, part * width + (at + 1) * LANES)
            total = wide_ref[0:1, cols] * padded[HALO : 2 * HALO, cols]
            for lag in range(1, TAPS):
                total = total + wide_ref[lag : lag + 1, cols] * padded[HALO - lag : 2 * HALO - lag, cols]
            parts.append(total)
        cot = cot_ref[:, at * LANES : (at + 1) * LANES].astype(F32)[:HALO]
        for index, array in enumerate(parts + [parts[1] * parts[2], cot * parts[0]]):
            first_rows[index, pl.ds(0, HALO, stride=8), :] = array
        for part in range(3):
            chunk = part * chunks + at
            feats_ref[chunk] = jnp.where(fresh_rows, first_rows[part, : 8 * HALO], feats_in[chunk])
        tiles = owner_tiles(first_rows[3].T, first_rows[4].T)
        here = slice(at * per_chunk, (at + 1) * per_chunk)
        for seq in range(4):
            out_ref[seq, here] = jnp.where(fresh, tiles[:, seq], sent_in[seq, here])


def gate_kernel(
    group_size,
    scale,
    got_ref,
    feats_ref,
    cot_ref,
    qkv_ref,
    rim_ref,
    mixer_hbm,
    gso_ref,
    edge_ref,
    short_ref,
    mixer_ref,
    stages,
    sums,
    sems,
):
    rows, width_all = qkv_ref.shape
    width = width_all // 3
    per_chunk = LANES // OWN // 4
    chunks = width // LANES

    def chunk(at, _):
        here = pl.ds(pl.multiple_of(at * LANES, LANES), LANES)
        both = jnp.stack(
            [got_ref[seq, pl.ds(at * per_chunk, per_chunk)] for seq in range(4)], axis=1
        ).astype(F32)
        both = both.reshape(LANES // OWN, 2 * OWN, LANES)
        long_out = both[:, :OWN].reshape(LANES, LANES).T
        grad_product = both[:, OWN:].reshape(LANES, LANES).T
        stages[3, HALO:, :] = cot_ref[:, here].astype(F32)
        mixed = feats_ref[at] * long_out
        mixer_ref[:, here] = unphased(stages.at[4, pl.ds(0, rows)], mixed).astype(BF16)
        grads = (
            phased(stages.at[3], 0, rows // 8) * long_out,
            grad_product * feats_ref[2 * chunks + at],
            grad_product * feats_ref[chunks + at],
        )
        for part in range(3):
            cols = pl.ds(pl.multiple_of(part * width + at * LANES, LANES), LANES)
            stages[part, 0:HALO, :] = rim_ref[:, cols].astype(F32)
            stages[part, HALO:, :] = qkv_ref[:, cols].astype(F32)
            shifted = phased(stages.at[part], 1 - TAPS, rows // 8 + TAPS - 1)
            gso_ref[part * chunks + at] = grads[part]
            edge_ref[:, cols] = gso_ref[part * chunks + at, pl.ds(0, HALO, stride=8), :].astype(BF16)
            for lag in range(TAPS):
                start = (TAPS - 1 - lag) * 8
                term = grads[part] * shifted[start : start + rows]
                sums[lag * 8 : (lag + 1) * 8, cols] = jnp.sum(
                    term.reshape(rows // 8, 8, LANES), axis=0
                )
        return 0

    per_copy = BLOCK // LANES
    copies = []
    for at in range(width // BLOCK):
        lax.fori_loop(at * per_copy, (at + 1) * per_copy, chunk, 0)
        copies.append(copy_out(mixer_ref, mixer_hbm, at, sems))
    span = LANES * group_size
    blocks = width_all // span
    lags = []
    for at in range(blocks):
        lags += [
            jnp.sum(sums[lag * 8 : (lag + 1) * 8, at * span : (at + 1) * span], axis=0, keepdims=True)
            for lag in range(TAPS)
        ]
        lags.append(jnp.zeros((8 - TAPS, span), F32))
    lags = jnp.concatenate(lags, axis=0)
    high = lags.astype(BF16)
    rest = lags - high.astype(F32)
    middle = rest.astype(BF16)
    low = (rest - middle.astype(F32)).astype(BF16)
    table = group_table(LANES, group_size).astype(BF16)
    dims = (((1,), (1,)), ((), ()))
    total = lax.dot_general(
        jnp.concatenate([high, middle, low], axis=0), table, dims, preferred_element_type=F32
    )
    count = blocks * 8
    total = total[:count] + (total[count : 2 * count] + total[2 * count :])
    for at in range(blocks):
        short_ref[:, at * LANES : (at + 1) * LANES] = total[at * 8 : (at + 1) * 8] * scale
    for copy in copies:
        copy.wait()


def copy_out(source, target, at, sems):
    cols = pl.ds(at * BLOCK, BLOCK)
    copy = pltpu.make_async_copy(source.at[:, cols], target.at[:, cols], sems.at[at])
    copy.start()
    return copy


def back_kernel(gso_ref, rim_ref, wide_ref, out_hbm, out_ref, last_rows, stage, sems):
    chunks, rows, _ = gso_ref.shape
    more = (TAPS - 1) * 8
    end = lax.broadcasted_iota(jnp.int32, (more, LANES), 0) % 8 == 7

    def chunk(at, _):
        cols = pl.ds(pl.multiple_of(at * LANES, LANES), LANES)
        last_rows[pl.ds(7, HALO, stride=8), :] = rim_ref[:, cols].astype(F32)
        here = gso_ref[at]
        after = jnp.where(end, last_rows[:more], gso_ref[at, 1 : more + 1])
        shifted = jnp.concatenate([here, after], axis=0)
        total = wide_ref[0:1, cols] * here
        for lag in range(1, TAPS):
            total = total + wide_ref[lag : lag + 1, cols] * shifted[lag * 8 : lag * 8 + rows]
        out_ref[:, cols] = unphased(stage, total).astype(BF16)
        return 0

    per_copy = BLOCK // LANES
    copies = []
    for at in range(chunks // per_copy):
        lax.fori_loop(at * per_copy, (at + 1) * per_copy, chunk, 0, unroll=2)
        copies.append(copy_out(out_ref, out_hbm, at, sems))
    for copy in copies:
        copy.wait()


def call(kernel, outs, scratch, args, cost, scalars=0, hbm_outs=()):
    vmem = pl.BlockSpec(memory_space=pltpu.VMEM)
    hbm = pl.BlockSpec(memory_space=pltpu.HBM)
    single = not isinstance(outs, tuple)
    outs = (outs,) if single else outs
    out_specs = tuple(hbm if at in hbm_outs else vmem for at in range(len(outs)))
    smem = pl.BlockSpec(memory_space=pltpu.SMEM)
    results = pl.pallas_call(
        kernel,
        out_shape=outs,
        in_specs=[smem] * scalars + [vmem] * (len(args) - scalars),
        out_specs=out_specs,
        scratch_shapes=scratch,
        compiler_params=pltpu.CompilerParams(vmem_limit_bytes=GRANT),
        cost_estimate=estimate(*cost),
    )(*args)
    return results[0] if single else results


def estimate(flops, moved):
    return pl.CostEstimate(flops=int(flops), bytes_accessed=int(moved), transcendentals=0)


def grid_call(kernel, steps, outs, out_specs, scratch, args, in_specs, cost, limit, aliases=None):
    return pl.pallas_call(
        kernel,
        grid=(steps,),
        out_shape=outs,
        in_specs=in_specs,
        out_specs=out_specs,
        scratch_shapes=scratch,
        input_output_aliases=aliases or {},
        compiler_params=pltpu.CompilerParams(vmem_limit_bytes=limit),
        cost_estimate=estimate(*cost),
    )(*args)


def shape(dims, kind):
    return jax.ShapeDtypeStruct(dims, kind)


def neighbours(array, by):
    devices = lax.axis_size("ctx")
    pairs = [(i, i + by) for i in range(devices) if 0 <= i + by < devices]
    return lax.ppermute(array, "ctx", pairs)


def partner(array, axis, mask):
    devices = lax.axis_size(axis)
    return lax.ppermute(array, axis, [(i, i ^ mask) for i in range(devices)])


def shards(qkv, short_filter, long_filter, cotangent):
    feats_in, cot = qkv[0], cotangent[0]
    rows, width_all = feats_in.shape
    width = width_all // 3
    tap_count, groups = short_filter.shape
    group_size = width_all // groups
    seqs, ctx_count = lax.axis_size("dp"), lax.axis_size("ctx")
    length = ctx_count * rows
    scale = 1.0 / math.sqrt(seqs * length)
    tables = make_tables(ctx_count, rows)
    place = lax.axis_index("dp").astype(jnp.int32).reshape(1)
    left_rim = neighbours(feats_in[rows - HALO :], 1)
    pair = (seqs, ctx_count, 2 * OWN, rows)
    vmem = pl.BlockSpec(memory_space=pltpu.VMEM)
    whole = lambda *dims: pl.BlockSpec(dims, lambda i: (0,) * len(dims))
    chunks = width_all // LANES
    feats_shape = shape((chunks, rows, LANES), F32)
    stages = lambda count: pltpu.VMEM((count, rows + HALO, LANES), F32)
    hbm = pl.BlockSpec(memory_space=pltpu.HBM)
    feats, sent, wide_taps = grid_call(
        functools.partial(short_kernel, group_size),
        1,
        (feats_shape, shape(pair, BF16), shape((8, width_all), F32)),
        (vmem, vmem, vmem),
        [
            pltpu.VMEM((tap_count, groups), F32),
            pltpu.VMEM((rows, width_all), BF16),
            pltpu.VMEM((rows, width), BF16),
            stages(8),
            pltpu.SemaphoreType.DMA((4 * width // BLOCK + 1,)),
        ],
        [pltpu.with_memory_space_constraint(arg, pltpu.HBM) for arg in (short_filter, feats_in, cot)],
        [hbm, hbm, hbm],
        (1e9, 6e6),
        FIRST_GRANT,
    )
    top = pl.BlockSpec((2 * HALO, width_all), lambda i: (0, 0))
    rows_top = pl.BlockSpec((chunks, 8 * HALO, LANES), lambda i: (0, 0, 0))
    feats, sent = grid_call(
        functools.partial(rim_kernel, width),
        1,
        (feats_shape, shape(pair, BF16)),
        (rows_top, whole(*pair)),
        [pltpu.VMEM((2 * HALO, width_all), F32), pltpu.VMEM((5, rows, LANES), F32)],
        (feats_in, left_rim, cot, wide_taps, feats, sent),
        [
            top,
            whole(HALO, width_all),
            pl.BlockSpec((2 * HALO, width), lambda i: (0, 0)),
            whole(8, width_all),
            rows_top,
            whole(*pair),
        ],
        (1e8, 2e6),
        GRANT,
        {4: 0, 5: 1},
    )
    sent, place = lax.optimization_barrier((sent, place))
    got = lax.all_to_all(
        sent.reshape(seqs * ctx_count, 2 * OWN, rows), ("dp", "ctx"), 0, 0, tiled=True
    ).reshape(pair)
    long_rows = pltpu.VMEM((seqs * ctx_count * 2 * OWN, rows), F32)
    spectra = (OWN, ctx_count, 2 * rows)
    mixed, own_taps = call(
        functools.partial(mix_kernel, seqs, ctx_count, scale),
        (shape(pair, BF16), shape((OWN, length), BF16)),
        [long_rows, long_rows, pltpu.VMEM(spectra, F32), pltpu.VMEM(spectra, F32)],
        (place, got, long_filter, *tables),
        (8e9, 6e6),
        1,
    )
    returned = lax.all_to_all(
        mixed.reshape(seqs * ctx_count, 2 * OWN, rows), ("dp", "ctx"), 0, 0, tiled=True
    ).reshape(pair)
    mixer_out, gso, edge, short_part = call(
        functools.partial(gate_kernel, group_size, scale),
        (
            shape((rows, width), BF16),
            feats_shape,
            shape((HALO, width_all), BF16),
            shape((8, groups), F32),
        ),
        [
            pltpu.VMEM((rows, width), BF16),
            stages(5),
            pltpu.VMEM((tap_count * 8, width_all), F32),
            pltpu.SemaphoreType.DMA((width // BLOCK,)),
        ],
        (returned, feats, cot, feats_in, left_rim),
        (1e9, 9e6),
        hbm_outs=(0,),
    )
    right_rim = neighbours(edge, -1)
    far = ctx_count // 2
    hops = [("ctx", 1), ("ctx", 2), ("ctx", 6), ("ctx", 8), ("ctx", 24)]
    hops += [(("dp", "ctx"), (seqs - 1) * ctx_count + far), ("dp", 1), ("dp", 2)]
    for at, (axis, mask) in enumerate(hops):
        if at == 2:
            own_taps, short_part = lax.optimization_barrier((own_taps, short_part))
            others = [partner(own_taps, "dp", step) for step in (1, 2, 3)]
        if at == 5:
            gso, right_rim, short_part = lax.optimization_barrier((gso, right_rim, short_part))
            grad_rows = call(
                back_kernel,
                shape((rows, width_all), BF16),
                [
                    pltpu.VMEM((rows, width_all), BF16),
                    pltpu.VMEM((8 * HALO, LANES), F32),
                    pltpu.VMEM((rows, LANES), F32),
                    pltpu.SemaphoreType.DMA((width_all // BLOCK,)),
                ],
                (gso, right_rim, wide_taps),
                (1e9, 6e6),
                hbm_outs=(0,),
            )
        if at == 7:
            others, short_part = lax.optimization_barrier((others, short_part))
            grad_long = call(
                join_kernel,
                shape((seqs * OWN, length), F32),
                [],
                (place, own_taps, *others),
                (1e8, 2e6),
                1,
            )
        short_part = short_part + partner(short_part, axis, mask)
        if at == 5:
            grad_rows, short_part = lax.optimization_barrier((grad_rows, short_part))
    return mixer_out[None], grad_rows[None], grad_long, short_part[:tap_count]


def solution(mesh):
    return jax.shard_map(
        shards,
        mesh=mesh,
        in_specs=(P("dp", "ctx", None), P(), P("ctx", None), P("dp", "ctx", None)),
        out_specs=(P("dp", "ctx", None), P("dp", "ctx", None), P("ctx", None), P()),
        check_vma=False,
    )
```
